32 devices in a mesh: ctx: 16 (over z, y, x), head: 2 (over core).
Axes of the slice: x: 2, y: 2, z: 4, core: 2. Of those that a mesh axis runs over, the one named last changes fastest.
Arguments:
- queries: bfloat16 [8192, 512], P('ctx', 'head'), may hold values from -12 to 12
- keys: bfloat16 [8192, 512], P('ctx', 'head'), may hold values from -12 to 12
- values: bfloat16 [8192, 1024], P('ctx', 'head'), may hold values from -6 to 6
- input_pre: float32 [8192, 2], P('ctx', 'head'), may hold values from -6 to 98
- forget_pre: float32 [8192, 2], P('ctx', 'head'), may hold values from -2 to 16
- output_pre: float32 [8192, 2], P('ctx', 'head'), may hold values from -8 to 8
- w_out: bfloat16 [1024, 1024], P('ctx', 'head'), may hold values from -0.25 to 0.25
Outputs:
- layer_out: bfloat16 [8192, 1024], P('ctx', 'head')
The draws below stay inside these ranges and needn't reach their ends.
All inputs are finite; a program needn't handle non-finite values.
Results may differ from the reference program's by a relative error of at most 0.0062.
Values may be sent and summed in bfloat16 or wider, within the bound.
No kernel may reach another device: no remote copies, remote signals or barrier semaphores. Data moves between devices by JAX's collectives and lax.ppermute only.
A program may use at most 128 MiB of HBM per device.

```python
import jax
import jax.numpy as jnp
from jax import lax

DK = 256
DV = 512
TOK_DEV = 512
MEMORY_HEADS = 2
D = 1024
SEQUENCE_TOKENS = 8192
N_CTX = 16


def shared_signs(key):
    return jnp.where(jax.random.normal(jax.random.fold_in(key, 77), (MEMORY_HEADS * DK,)) > 0.0, 1.0, -1.0)


def quiet_heads(key):
    order = jax.random.permutation(jax.random.fold_in(key, 59), MEMORY_HEADS)
    return order < max(1, MEMORY_HEADS // 4)


def noisy_rows(key, salt):
    signs = shared_signs(key)
    inner = jax.random.fold_in(key, salt)
    noise = jnp.clip(jax.random.normal(inner, (SEQUENCE_TOKENS, MEMORY_HEADS * DK)), -4.0, 4.0)
    loud_cols = jnp.repeat(jnp.where(quiet_heads(key), 0.0, 1.0), DK)
    shift = 0.35 * signs * loud_cols
    return (noise + shift[None, :]).astype(jnp.bfloat16)


def draw_queries(key, part):
    return noisy_rows(key, 1)


def draw_keys(key, part):
    return noisy_rows(key, 2)


def draw_input_pre(key, part):
    inner = jax.random.fold_in(key, 31)
    base = jnp.clip(1.5 * jax.random.normal(inner, (SEQUENCE_TOKENS, MEMORY_HEADS)), -6.0, 6.0)
    level = jax.random.uniform(jax.random.fold_in(inner, 5), (MEMORY_HEADS,), minval=-5.5, maxval=-3.5)
    low = jnp.clip(level[None, :] + 0.5 * jax.random.normal(jax.random.fold_in(inner, 7), (SEQUENCE_TOKENS, MEMORY_HEADS)), -6.0, 6.0)
    return jnp.where(quiet_heads(key)[None, :], low, base)


def draw_forget_pre(key, part):
    base = jax.random.fold_in(key, 101)
    every_key_row = jax.random.split(base, 7)
    fast_share = 0.5
    is_fast = jax.random.uniform(every_key_row[0], (MEMORY_HEADS,)) < fast_share
    fast_rate = jnp.exp(jax.random.uniform(every_key_row[1], (MEMORY_HEADS,), minval=jnp.log(1.0 / 50.0), maxval=jnp.log(1.0 / 30.0)))
    slow_rate = jnp.exp(jax.random.uniform(every_key_row[2], (MEMORY_HEADS,), minval=jnp.log(0.1), maxval=jnp.log(0.8))) / SEQUENCE_TOKENS
    rate = jnp.where(is_fast, fast_rate, slow_rate)
    blocks = SEQUENCE_TOKENS // TOK_DEV
    block_factor = jnp.exp(jax.random.uniform(every_key_row[3], (blocks, 1, MEMORY_HEADS), minval=jnp.log(0.5), maxval=jnp.log(2.0)))
    token_factor = jax.random.uniform(every_key_row[4], (blocks, TOK_DEV, MEMORY_HEADS), minval=0.5, maxval=1.5)
    log_forget_gate = -(rate[None, None, :] * block_factor * token_factor).reshape(SEQUENCE_TOKENS, MEMORY_HEADS)
    spots = jax.random.randint(every_key_row[5], (3,), 0, SEQUENCE_TOKENS)
    masked_entries = jnp.any(jnp.arange(SEQUENCE_TOKENS)[:, None] == spots[None, :], axis=1)
    spike_penalty = jax.random.uniform(every_key_row[6], (SEQUENCE_TOKENS, MEMORY_HEADS), minval=0.22, maxval=0.51)
    log_forget_gate = log_forget_gate - jnp.where(masked_entries[:, None], spike_penalty, 0.0)
    return log_forget_gate - jnp.log(-jnp.expm1(log_forget_gate))


def spiked(entries, own_key, source, target, parts, factor):
    def block_of(axis_at):
        return (jnp.arange(entries.shape[axis_at]) // (entries.shape[axis_at] // parts)).reshape((-1,) + (1,) * (entries.ndim - 1 - axis_at))

    first = jax.random.permutation(own_key, parts)[block_of(target)]
    other_side = (block_of(target) + parts // 2) % parts
    return jnp.where((block_of(source) == first) | (block_of(source) == other_side), factor * entries, entries)


def level_of(stream_key, dims, shards, smallest, high):
    loudness = 1.0
    for axis_at, parts in shards:
        heights = jax.random.uniform(jax.random.fold_in(jax.random.fold_in(stream_key, 6), axis_at), (parts,), jnp.float32, smallest / len(shards), high / len(shards))
        loudness = loudness * jnp.repeat(jnp.exp(heights), dims[axis_at] // parts).reshape((-1,) + (1,) * (len(dims) - 1 - axis_at))
    return loudness


def scatter_about(key, extent, scale, limit, shards=(), dtype=jnp.bfloat16):
    factor_of = level_of(key, extent, shards, -0.22, 0.18) if shards else 1.0
    entries = jax.random.normal(key, extent, jnp.float32) * scale * factor_of
    return jnp.minimum(jnp.maximum(entries, -limit), limit).astype(dtype)


def bell_draw_with(key, extent, scale, bound, pieces, heavy, kind=jnp.bfloat16):
    values = scale * jax.random.normal(key, extent, jnp.float32)
    if pieces:
        values = values * level_of(key, extent, pieces, -0.22, 0.18)
    return jnp.clip(spiked(values, jax.random.fold_in(key, 3), *heavy), -bound, bound).astype(kind)


def setup_inputs(seed: int = 0) -> dict:
    key_list = jax.random.split(jax.random.key(seed), 8)
    return {
        "queries": draw_queries(jax.random.fold_in(key_list[7], 71), 0),
        "keys": draw_keys(jax.random.fold_in(key_list[7], 71), 0),
        "values": scatter_about(key_list[2], (SEQUENCE_TOKENS, MEMORY_HEADS * DV), 1.0, 6.0, ((0, 16), (1, 2))),
        "input_pre": draw_input_pre(jax.random.fold_in(key_list[7], 71), 0),
        "forget_pre": draw_forget_pre(jax.random.fold_in(key_list[7], 71), 0),
        "output_pre": scatter_about(key_list[5], (SEQUENCE_TOKENS, MEMORY_HEADS), 1.5, 8.0, ((0, 16), (1, 2)), jnp.float32),
        "w_out": bell_draw_with(key_list[6], (D, D), D ** -0.5, 0.25, ((0, 16), (1, 2)), (0, 1, 16, 2.0)),
    }


def combine(earlier, later):
    mem_a, norm_a, top_a, decay_a = earlier
    mem_b, norm_b, top_b, decay_b = later
    top_log = jnp.maximum(decay_b + top_a, top_b)
    keep_old = jnp.exp(decay_b + top_a - top_log)
    fresh_w = jnp.exp(top_b - top_log)
    return (keep_old * mem_a + fresh_w * mem_b, keep_old * norm_a + fresh_w * norm_b, top_log, decay_a + decay_b)


def block_pass(query_b, key_b, value_b, forget_b, input_b, outgate_b, carried):
    memory, norm_vec, top_prev = carried
    tok_rows = query_b.shape[0]
    score_scale = DK ** -0.5
    log_forget_gate = jax.nn.log_sigmoid(forget_b)
    cum_decay = jnp.cumsum(log_forget_gate)
    block_decay = cum_decay[-1]
    rest_gain = block_decay - cum_decay + input_b
    top_local = jnp.max(rest_gain)
    key_weight = jnp.exp(rest_gain - top_local)
    scaled = key_b.astype(jnp.float32) * key_weight[:, None]
    memory_local = jnp.dot(scaled.astype(jnp.bfloat16).T, value_b, preferred_element_type=jnp.float32)
    norm_local = jnp.sum(scaled, axis=0)
    scores = jnp.dot(query_b, key_b.T, preferred_element_type=jnp.float32) * score_scale
    causal = jnp.arange(tok_rows)[:, None] >= jnp.arange(tok_rows)[None, :]
    rel_gain = jnp.where(causal, cum_decay[:, None] - cum_decay[None, :] + input_b[None, :], -1e30)
    top_tok = jnp.maximum(cum_decay + top_prev, jnp.max(rel_gain, axis=1))
    weighted = jnp.exp(rel_gain - top_tok[:, None]) * scores
    den_in = jnp.sum(weighted, axis=1)
    numerator_input = jnp.dot(weighted.astype(jnp.bfloat16), value_b, preferred_element_type=jnp.float32)
    lift = jnp.exp(cum_decay + top_prev - top_tok)
    num_out = jnp.dot(query_b, memory.astype(jnp.bfloat16), preferred_element_type=jnp.float32) * score_scale
    normalizer_output = jnp.dot(query_b.astype(jnp.float32), norm_vec, precision=lax.Precision.HIGHEST) * score_scale
    numer = numerator_input + lift[:, None] * num_out
    denom = jnp.maximum(jnp.abs(den_in + lift * normalizer_output), jnp.exp(-top_tok))
    hidden = numer / denom[:, None]
    gated_out = (jax.nn.sigmoid(outgate_b)[:, None] * hidden).astype(jnp.bfloat16)
    state_next = combine((memory, norm_vec, top_prev, jnp.zeros((), jnp.float32)), (memory_local, norm_local, top_local, block_decay))
    return state_next[:3], gated_out


def one_head(inputs):
    query_h, key_h, value_h, forget_h, input_h, outgate_h = inputs
    start_state = (jnp.zeros((DK, DV), jnp.float32), jnp.zeros((DK,), jnp.float32), jnp.array(-1e30, jnp.float32))

    def advance(carried, block_in):
        return block_pass(*block_in, carried)

    _, outputs = lax.scan(advance, start_state, (query_h, key_h, value_h, forget_h, input_h, outgate_h))
    return outputs


def split_heads(array, width):
    return array.reshape(SEQUENCE_TOKENS, MEMORY_HEADS, width).transpose(1, 0, 2).reshape(MEMORY_HEADS, N_CTX, TOK_DEV, width)


def split_gates(array):
    return array.T.reshape(MEMORY_HEADS, N_CTX, TOK_DEV)


def reference(queries, keys, values, input_pre, forget_pre, output_pre, w_out):
    gated_heads = lax.map(one_head, (split_heads(queries, DK), split_heads(keys, DK), split_heads(values, DV), split_gates(forget_pre), split_gates(input_pre), split_gates(output_pre)))
    gated_all = gated_heads.reshape(MEMORY_HEADS, SEQUENCE_TOKENS, DV).transpose(1, 0, 2).reshape(SEQUENCE_TOKENS, D)
    return jnp.dot(gated_all, w_out, preferred_element_type=jnp.float32).astype(jnp.bfloat16)
```

```python
import functools

import jax
import jax.numpy as jnp
from jax import lax
from jax.experimental import pallas as pl
from jax.experimental.pallas import tpu as pltpu
from jax.sharding import PartitionSpec as P

AUX = 16
LANES = 128
NEG = -1e30


def split_groups(n):
    inner = max(a for a in range(1, n + 1) if n % a == 0 and a * a <= n)
    return inner, n // inner


def is_pow2(n):
    return n & (n - 1) == 0


def source(i, k, n):
    return i ^ k if is_pow2(n) else (i + k) % n


def target(i, k, n):
    return i ^ k if is_pow2(n) else (i + n - k) % n


def inner_pairs(n, inner, k):
    return [(j, j - j % inner + target(j % inner, k, inner)) for j in range(n)]


def outer_pairs(n, inner, k):
    outer = n // inner
    return [(j, target(j // inner, k, outer) * inner + j % inner) for j in range(n)]


def pieces3(x):
    hi = x.astype(jnp.bfloat16)
    rest = x - hi.astype(jnp.float32)
    mid = rest.astype(jnp.bfloat16)
    low = (rest - mid.astype(jnp.float32)).astype(jnp.bfloat16)
    return hi, mid, low


def write_aux(ref, at, norm, top, decay):
    lanes = ref.shape[1]
    pad = jnp.zeros((1, lanes - norm.shape[1]), jnp.float32)
    norm = jnp.concatenate([norm, pad], axis=1) if lanes > norm.shape[1] else norm
    wide = [jnp.broadcast_to(x, (1, lanes)) for x in (norm, top, decay)]
    rows = [p.astype(jnp.float32) for x in wide for p in pieces3(x)]
    rows.append(jnp.zeros((AUX - len(rows), lanes), jnp.float32))
    ref[pl.ds(at, AUX), :] = jnp.concatenate(rows, axis=0).astype(jnp.bfloat16)


def read_aux(ref, at):
    aux = ref[pl.ds(at, AUX), :].astype(jnp.float32)
    return [aux[i : i + 1] + aux[i + 1 : i + 2] + aux[i + 2 : i + 3] for i in (0, 3, 6)]


def summary_kernel(inner, forget_ref, input_ref, keys_ref, values_ref, *rest):
    gates_ref, outs, memory = rest[0], rest[1:-1], rest[-1]
    member = lax.rem(lax.axis_index("ctx"), inner)
    rows = forget_ref.shape[0]
    forget = forget_ref[...]
    log_keep = jnp.minimum(forget, 0.0) - jnp.log1p(jnp.exp(-jnp.abs(forget)))
    tri = lax.broadcasted_iota(jnp.int32, (LANES, LANES), 0) <= lax.broadcasted_iota(
        jnp.int32, (LANES, LANES), 1
    )
    parts = jnp.concatenate([p.astype(jnp.float32) for p in pieces3(log_keep)], axis=0)
    sums = jnp.dot(
        parts.astype(jnp.bfloat16),
        tri.astype(jnp.bfloat16),
        preferred_element_type=jnp.float32,
    )
    inside = sums[:rows] + sums[rows : 2 * rows] + sums[2 * rows : 3 * rows]
    base = jnp.zeros((1, 1), jnp.float32)
    cum = []
    for r in range(rows):
        row = inside[r : r + 1]
        cum.append(row + base)
        base = base + row[:, LANES - 1 :]
    cum_decay = jnp.concatenate(cum, axis=0)
    gain = input_ref[...] - cum_decay
    top_gain = jnp.max(jnp.max(gain, axis=1, keepdims=True), axis=0, keepdims=True)
    weight = jnp.exp(gain - top_gain)
    gates_ref[0:rows, :] = gain
    gates_ref[rows : 2 * rows, :] = cum_decay
    along = jnp.concatenate([weight[r : r + 1] for r in range(rows)], axis=1)
    keys = keys_ref[...]
    scaled = (keys.astype(jnp.float32).T * along).astype(jnp.bfloat16)
    memory[...] = jnp.dot(scaled, values_ref[...], preferred_element_type=jnp.float32)
    three = [p.astype(jnp.float32) for p in pieces3(along)]
    three.append(jnp.zeros((AUX - 3, along.shape[1]), jnp.float32))
    norms = jnp.dot(
        jnp.concatenate(three, axis=0).astype(jnp.bfloat16),
        keys,
        preferred_element_type=jnp.float32,
    )
    norm = norms[0:1] + norms[1:2] + norms[2:3]
    piece = memory.shape[0] // inner
    for k, out_ref in enumerate(outs):
        start = pl.multiple_of(target(member, k, inner) * piece, piece)
        out_ref[0:piece, :] = memory[pl.ds(start, piece), :].astype(jnp.bfloat16)
        write_aux(out_ref, piece, norm, base + top_gain, base)


def group_total_kernel(inner, *refs):
    ins, out_ref = refs[:-1], refs[-1]
    member = lax.rem(lax.axis_index("ctx"), inner)
    piece = out_ref.shape[0] - AUX
    where = [source(member, k, inner) for k in range(inner)]
    norms, tops, decays = zip(*[read_aux(r, piece) for r in ins])
    logs = []
    for k in range(inner):
        log = tops[k]
        for o in range(inner):
            if o != k:
                log = log + jnp.where(where[o] > where[k], decays[o], 0.0)
        logs.append(log)
    top = functools.reduce(jnp.maximum, logs)
    total, norm = 0.0, 0.0
    for k in range(inner):
        weight = jnp.exp(logs[k] - top)
        total = total + weight * ins[k][0:piece, :].astype(jnp.float32)
        norm = norm + weight * norms[k]
    out_ref[0:piece, :] = total.astype(jnp.bfloat16)
    write_aux(out_ref, piece, norm, top, functools.reduce(jnp.add, decays))


def prefix_kernel(inner, outer, *refs):
    blocks, totals = refs[:inner], refs[inner : inner + outer - 1]
    outs, state_ref = refs[inner + outer - 1 : -1], refs[-1]
    place = lax.axis_index("ctx")
    member, group = lax.rem(place, inner), lax.div(place, inner)
    piece = blocks[0].shape[0] - AUX
    at = [source(group, k, outer) for k in range(1, outer)]
    t_norm, t_top, t_decay = zip(*[read_aux(r, piece) for r in totals])
    logs = []
    for k in range(outer - 1):
        log = t_top[k]
        for o in range(outer - 1):
            if o != k:
                between = jnp.logical_and(at[o] > at[k], at[o] < group)
                log = log + jnp.where(between, t_decay[o], 0.0)
        logs.append(jnp.where(at[k] < group, log, NEG))
    far_top = functools.reduce(jnp.maximum, logs)
    far, far_norm = 0.0, 0.0
    for k in range(outer - 1):
        weight = jnp.where(at[k] < group, jnp.exp(logs[k] - far_top), 0.0)
        far = far + weight * totals[k][0:piece, :].astype(jnp.float32)
        far_norm = far_norm + weight * t_norm[k]
    where = [source(member, k, inner) for k in range(inner)]
    norms, tops, decays = zip(*[read_aux(r, piece) for r in blocks])
    for t in range(inner):
        end = target(member, t, inner)
        far_log = far_top
        for o in range(inner):
            far_log = far_log + jnp.where(where[o] < end, decays[o], 0.0)
        logs = []
        for k in range(inner):
            log = tops[k]
            for o in range(inner):
                if o != k:
                    between = jnp.logical_and(where[o] > where[k], where[o] < end)
                    log = log + jnp.where(between, decays[o], 0.0)
            logs.append(jnp.where(where[k] < end, log, NEG))
        top = jnp.maximum(functools.reduce(jnp.maximum, logs), far_log)
        top = jnp.maximum(top, NEG)
        weight = jnp.exp(far_log - top)
        memory, norm = weight * far, weight * far_norm
        for k in range(inner):
            weight = jnp.where(where[k] < end, jnp.exp(logs[k] - top), 0.0)
            memory = memory + weight * blocks[k][0:piece, :].astype(jnp.float32)
            norm = norm + weight * norms[k]
        outs[t][...] = memory.astype(jnp.bfloat16)
        if t == 0:
            lanes = state_ref.shape[1]
            pad = jnp.zeros((6, lanes), jnp.float32)
            state_ref[...] = jnp.concatenate([top, norm, pad], axis=0)


def inside_kernel(gates_ref, output_ref, queries_ref, keys_ref, values_ref, num_ref, cols_ref):
    rows = output_ref.shape[0]
    scale = queries_ref.shape[1] ** (-0.5)
    down = lax.broadcasted_iota(jnp.int32, (LANES, LANES), 0)
    across = lax.broadcasted_iota(jnp.int32, (LANES, LANES), 1)
    causal, same = down >= across, down == across
    lane = lax.broadcasted_iota(jnp.int32, (LANES, LANES), 1)
    gain = gates_ref[0:rows, :]
    cum_decay = gates_ref[rows : 2 * rows, :]
    open_gate = jax.nn.sigmoid(output_ref[...])

    def column(row):
        return jnp.sum(jnp.where(same, row, 0.0), axis=1, keepdims=True)

    before = jnp.full((1, 1), NEG, jnp.float32)
    for i in range(rows):
        here = slice(i * LANES, (i + 1) * LANES)
        a_row = gain[i : i + 1]
        peak = jnp.max(jnp.where(causal, a_row, NEG), axis=1, keepdims=True)
        peak = jnp.maximum(peak, before)
        before = jnp.maximum(before, jnp.max(a_row, axis=1, keepdims=True))
        width = (i + 1) * LANES
        scores = lax.dot_general(
            queries_ref[here, :],
            keys_ref[0:width, :],
            (((1,), (1,)), ((), ())),
            preferred_element_type=jnp.float32,
        )
        parts, den = [], 0.0
        for j in range(i + 1):
            diff = gain[j : j + 1] - peak
            if j == i:
                diff = jnp.where(causal, diff, NEG)
            part = jnp.exp(diff) * (scores[:, j * LANES : (j + 1) * LANES] * scale)
            den = den + part
            parts.append(part.astype(jnp.bfloat16))
        weighted = parts[0] if i == 0 else jnp.concatenate(parts, axis=1)
        den = jnp.sum(den, axis=1, keepdims=True)
        num_ref[here, :] = jnp.dot(
            weighted, values_ref[0:width, :], preferred_element_type=jnp.float32
        )
        cols = jnp.where(lane == 0, den, peak)
        cols = jnp.where(lane == 2, column(cum_decay[i : i + 1]), cols)
        cols_ref[here, :] = jnp.where(lane == 3, column(open_gate[i : i + 1]), cols)


def output_kernel(inner, state_ref, queries_ref, num_ref, cols_ref, *rest):
    pieces, out_ref, memory = rest[:inner], rest[inner], rest[inner + 1]
    member = lax.rem(lax.axis_index("ctx"), inner)
    piece = pieces[0].shape[0]
    for k in range(inner):
        start = pl.multiple_of(source(member, k, inner) * piece, piece)
        memory[pl.ds(start, piece), :] = pieces[k][...]
    width = queries_ref.shape[1]
    scale = width ** (-0.5)
    top_prev = state_ref[0:1, 0:1]
    norm = state_ref[1:2, 0:width]
    step = LANES
    for i in range(queries_ref.shape[0] // step):
        here = slice(i * step, (i + 1) * step)
        q = queries_ref[here, :]
        num_out = jnp.dot(q, memory[...], preferred_element_type=jnp.float32)
        den_out = jnp.sum(q.astype(jnp.float32) * norm, axis=1, keepdims=True)
        cols = cols_ref[here, :]
        den_in, peak = cols[:, 0:1], cols[:, 1:2]
        cum_decay, open_gate = cols[:, 2:3], cols[:, 3:4]
        top = jnp.maximum(peak, top_prev)
        keep, lift = jnp.exp(peak - top), jnp.exp(top_prev - top) * scale
        den = jnp.abs(keep * den_in + lift * den_out)
        ratio = open_gate / jnp.maximum(den, jnp.exp(-(cum_decay + top)))
        gated = (keep * ratio) * num_ref[here, :] + (lift * ratio) * num_out
        out_ref[here, :] = gated.astype(jnp.bfloat16)


def project_kernel(heads, order, rows, *refs):
    gated, bufs = refs[:heads], refs[heads:-2]
    out_ref, weights = refs[-2], refs[-1]
    place, head = lax.axis_index("ctx"), lax.axis_index("head")
    at = 0
    for buf in bufs:
        for s in range(buf.shape[0] // rows):
            block = place ^ order[at] if order is not None else at
            start = pl.multiple_of(block * rows, rows)
            weights[pl.ds(start, rows), :] = buf[s * rows : (s + 1) * rows, :]
            at += 1
    width = gated[0].shape[1]
    total = 0.0
    for k in range(heads):
        start = pl.multiple_of(source(head, k, heads) * width, width)
        total = total + jnp.dot(
            gated[k][...], weights[pl.ds(start, width), :], preferred_element_type=jnp.float32
        )
    out_ref[...] = total.astype(jnp.bfloat16)


def call(kernel, out_shape, args, scratch=(), flops=0, moved=0):
    return pl.pallas_call(
        kernel,
        out_shape=out_shape,
        in_specs=[pl.BlockSpec(memory_space=pltpu.VMEM)] * len(args),
        out_specs=jax.tree.map(lambda _: pl.BlockSpec(memory_space=pltpu.VMEM), out_shape),
        scratch_shapes=scratch,
        compiler_params=pltpu.CompilerParams(vmem_limit_bytes=24 * 2**20),
        cost_estimate=pl.CostEstimate(flops=flops, bytes_accessed=moved, transcendentals=0),
    )(*args)


def shape(dims, dtype):
    return jax.ShapeDtypeStruct(dims, dtype)


def local(n_ctx, n_head, queries, keys, values, input_pre, forget_pre, output_pre, w_out):
    tok, width_k = queries.shape
    width_v = values.shape[1]
    inner, outer = split_groups(n_ctx)
    piece = width_k // inner
    bf16, f32 = jnp.bfloat16, jnp.float32
    gate_rows = tok // LANES
    forget, gate_in, gate_out = (
        g.reshape(gate_rows, LANES) for g in (forget_pre, input_pre, output_pre)
    )

    steps = [1 << b for b in reversed(range(n_ctx.bit_length() - 1))] if is_pow2(n_ctx) else []
    order = [0] if is_pow2(n_ctx) else None
    w_held, w_bufs = w_out, [w_out]
    for i, s in enumerate(steps):
        got = lax.ppermute(w_held, "ctx", [(j, j ^ s) for j in range(n_ctx)])
        order = order + [o ^ s for o in order]
        w_bufs = [w_held, got]
        if i < len(steps) - 1:
            w_held = jnp.concatenate(w_bufs, axis=0)
    if order is None:
        w_bufs = [lax.all_gather(w_out, "ctx", axis=0, tiled=True)]

    message = shape((piece + AUX, width_v), bf16)
    gates, *sends = call(
        functools.partial(summary_kernel, inner),
        [shape((2 * gate_rows, LANES), f32)] + [message] * inner,
        (forget, gate_in, keys, values),
        [pltpu.VMEM((width_k, width_v), f32)],
        2 * tok * width_k * width_v,
        2 * tok * (width_k + width_v),
    )
    blocks = [sends[0]] + [
        lax.ppermute(sends[k], "ctx", inner_pairs(n_ctx, inner, k)) for k in range(1, inner)
    ]
    num_in, cols = call(
        inside_kernel,
        [shape((tok, width_v), f32), shape((tok, LANES), f32)],
        (gates, gate_out, queries, keys, values),
        (),
        2 * tok * tok * (width_k + width_v),
        2 * tok * (2 * width_k + 3 * width_v),
    )
    total = call(functools.partial(group_total_kernel, inner), message, blocks)
    totals = [
        lax.ppermute(total, "ctx", outer_pairs(n_ctx, inner, k)) for k in range(1, outer)
    ]
    *prefixes, state = call(
        functools.partial(prefix_kernel, inner, outer),
        [shape((piece, width_v), bf16)] * inner + [shape((8, width_v), f32)],
        (*blocks, *totals),
    )
    parts = [prefixes[0]] + [
        lax.ppermute(prefixes[k], "ctx", inner_pairs(n_ctx, inner, k)) for k in range(1, inner)
    ]
    gated = call(
        functools.partial(output_kernel, inner),
        shape((tok, width_v), bf16),
        (state, queries, num_in, cols, *parts),
        [pltpu.VMEM((width_k, width_v), bf16)],
        2 * tok * width_k * width_v,
    )
    others = [
        lax.ppermute(gated, "head", [(j, target(j, k, n_head)) for j in range(n_head)])
        for k in range(1, n_head)
    ]
    return call(
        functools.partial(project_kernel, n_head, order, w_out.shape[0]),
        shape((tok, w_out.shape[1]), bf16),
        (gated, *others, *w_bufs),
        [pltpu.VMEM((n_ctx * w_out.shape[0], w_out.shape[1]), bf16)],
    )


def solution(mesh):
    spec = P("ctx", "head")
    return jax.shard_map(
        functools.partial(local, mesh.shape["ctx"], mesh.shape["head"]),
        mesh=mesh,
        in_specs=(spec,) * 7,
        out_specs=spec,
        check_vma=False,
    )
```

```python
import functools

import jax
import jax.numpy as jnp
from jax import lax
from jax.experimental import pallas as pl
from jax.experimental.pallas import tpu as pltpu
from jax.sharding import PartitionSpec as P

TILE = 16
LANES = 128
NEG = -1e30


def split_groups(n):
    inner = max(a for a in range(1, n + 1) if n % a == 0 and a * a <= n)
    return inner, n // inner


def is_pow2(n):
    return n & (n - 1) == 0


def source(i, k, n):
    return i ^ k if is_pow2(n) else (i + k) % n


def target(i, k, n):
    return i ^ k if is_pow2(n) else (i + n - k) % n


def inner_pairs(n, inner, k):
    return [(j, j - j % inner + target(j % inner, k, inner)) for j in range(n)]


def outer_pairs(n, inner, k):
    outer = n // inner
    return [(j, target(j // inner, k, outer) * inner + j % inner) for j in range(n)]


def pieces3(x):
    hi = x.astype(jnp.bfloat16)
    rest = x - hi.astype(jnp.float32)
    mid = rest.astype(jnp.bfloat16)
    low = (rest - mid.astype(jnp.float32)).astype(jnp.bfloat16)
    return hi, mid, low


def lane_blocks(x):
    return [x[:, i : i + LANES] for i in range(0, x.shape[1], LANES)]


def rows_for(width_k):
    rows = 3 * (width_k // LANES + 2)
    return rows + -rows % TILE


def write_tail(ref, at, norm, top, decay):
    wide = jnp.concatenate([norm] + [jnp.broadcast_to(x, (1, LANES)) for x in (top, decay)], axis=0)
    rows = [p.astype(jnp.float32) for p in pieces3(wide)]
    count = ref.shape[0] - at - 3 * wide.shape[0]
    if count:
        rows.append(jnp.zeros((count, LANES), jnp.float32))
    ref[at:, :] = jnp.concatenate(rows, axis=0).astype(jnp.bfloat16)


def read_tail(ref, at, width_k):
    tail = ref[at:, :].astype(jnp.float32)
    n = width_k // LANES
    tail = tail[0 : n + 2] + tail[n + 2 : 2 * n + 4] + tail[2 * n + 4 : 3 * n + 6]
    return tail[0:n], tail[n : n + 1], tail[n + 1 : n + 2]


def read_tails(refs, width_k):
    at = refs[0].shape[0] - rows_for(width_k)
    return at, zip(*[read_tail(r, at, width_k) for r in refs])


def summary_kernel(inner, *refs):
    given, gates_ref, outs = refs[:4], refs[4], refs[5 : 5 + inner]
    memory, sems = refs[5 + inner], refs[-1]
    held = forget_ref, input_ref, keys_ref, values_ref = refs[6 + inner : -1]
    copies = [
        pltpu.make_async_copy(src, dst, sems.at[i]) for i, (src, dst) in enumerate(zip(given, held))
    ]
    for copy in copies:
        copy.start()
    copies[0].wait()
    copies[1].wait()
    member = lax.rem(lax.axis_index("ctx"), inner)
    rows = forget_ref.shape[0]
    forget = forget_ref[...]
    log_keep = jnp.minimum(forget, 0.0) - jnp.log1p(jnp.exp(-jnp.abs(forget)))
    tri = lax.broadcasted_iota(jnp.int32, (LANES, LANES), 0) <= lax.broadcasted_iota(
        jnp.int32, (LANES, LANES), 1
    )
    parts = jnp.concatenate([p.astype(jnp.float32) for p in pieces3(log_keep)], axis=0)
    sums = jnp.dot(
        parts.astype(jnp.bfloat16),
        tri.astype(jnp.bfloat16),
        preferred_element_type=jnp.float32,
    )
    inside = sums[:rows] + sums[rows : 2 * rows] + sums[2 * rows : 3 * rows]
    base = jnp.zeros((1, 1), jnp.float32)
    cum = []
    for r in range(rows):
        row = inside[r : r + 1]
        cum.append(row + base)
        base = base + row[:, LANES - 1 :]
    cum_decay = jnp.concatenate(cum, axis=0)
    gain = input_ref[...] - cum_decay
    top_gain = jnp.max(jnp.max(gain, axis=1, keepdims=True), axis=0, keepdims=True)
    weight = jnp.exp(gain - top_gain)
    gates_ref[0:rows, :] = gain
    gates_ref[rows : 2 * rows, :] = cum_decay
    along = jnp.concatenate([weight[r : r + 1] for r in range(rows)], axis=1)
    three = [p.astype(jnp.float32) for p in pieces3(along)]
    three.append(jnp.zeros((TILE - 3, along.shape[1]), jnp.float32))
    three = jnp.concatenate(three, axis=0).astype(jnp.bfloat16)
    copies[2].wait()
    keys = keys_ref[...]
    scaled = (keys.astype(jnp.float32).T * along).astype(jnp.bfloat16)
    norms = jnp.dot(three, keys, preferred_element_type=jnp.float32)
    norm = jnp.concatenate(lane_blocks(norms[0:1] + norms[1:2] + norms[2:3]), axis=0)
    copies[3].wait()
    memory[...] = jnp.dot(scaled, values_ref[...], preferred_element_type=jnp.float32)
    piece = memory.shape[0] // inner
    for k, out_ref in enumerate(outs):
        start = pl.multiple_of(target(member, k, inner) * piece, piece)
        wide = memory[pl.ds(start, piece), :].astype(jnp.bfloat16)
        for i, block in enumerate(lane_blocks(wide)):
            out_ref[i * piece : (i + 1) * piece, :] = block
        write_tail(out_ref, wide.size // LANES, norm, base + top_gain, base)


def chain_logs(where, tops, decays, end):
    logs = []
    for k in range(len(where)):
        log = tops[k]
        for o in range(len(where)):
            if o != k:
                between = jnp.logical_and(where[o] > where[k], where[o] < end)
                log = log + jnp.where(between, decays[o], 0.0)
        logs.append(jnp.where(where[k] < end, log, NEG))
    return logs


def chain_sum(where, logs, top, end, refs, at, norms):
    total, norm = 0.0, 0.0
    for k in range(len(where)):
        weight = jnp.where(where[k] < end, jnp.exp(logs[k] - top), 0.0)
        total = total + weight * refs[k][0:at, :].astype(jnp.float32)
        norm = norm + weight * norms[k]
    return total, norm


def group_total_kernel(inner, width_k, *refs):
    ins, out_ref = refs[:-1], refs[-1]
    member = lax.rem(lax.axis_index("ctx"), inner)
    where = [source(member, k, inner) for k in range(inner)]
    at, (norms, tops, decays) = read_tails(ins, width_k)
    logs = chain_logs(where, tops, decays, inner)
    top = functools.reduce(jnp.maximum, logs)
    total, norm = chain_sum(where, logs, top, inner, ins, at, norms)
    out_ref[0:at, :] = total.astype(jnp.bfloat16)
    write_tail(out_ref, at, norm, top, functools.reduce(jnp.add, decays))


def near_kernel(inner, width_k, *refs):
    ins, outs, stats_ref = refs[:inner], refs[inner:-1], refs[-1]
    member = lax.rem(lax.axis_index("ctx"), inner)
    where = [source(member, k, inner) for k in range(inner)]
    at, (norms, tops, decays) = read_tails(ins, width_k)
    for t in range(inner):
        end = target(member, t, inner)
        logs = chain_logs(where, tops, decays, end)
        top = functools.reduce(jnp.maximum, logs)
        total, norm = chain_sum(where, logs, top, end, ins, at, norms)
        outs[t][...] = total
        decay = 0.0
        for k in range(inner):
            decay = decay + jnp.where(where[k] < end, decays[k], 0.0)
        pad = jnp.zeros((8 - norm.shape[0] % 8 - 2, LANES), jnp.float32)
        stats_ref[t, :, :] = jnp.concatenate([top, decay, norm, pad], axis=0)


def far_kernel(inner, outer, width_k, stats_ref, *refs):
    totals, nears = refs[: outer - 1], refs[outer - 1 : outer - 1 + inner]
    outs, state_ref = refs[outer - 1 + inner : -1], refs[-1]
    group = lax.div(lax.axis_index("ctx"), inner)
    where = [source(group, k, outer) for k in range(1, outer)]
    at, (norms, tops, decays) = read_tails(totals, width_k)
    logs = chain_logs(where, tops, decays, group)
    far_top = functools.reduce(jnp.maximum, logs)
    far, far_norm = chain_sum(where, logs, far_top, group, totals, at, norms)
    n = width_k // LANES
    for t in range(inner):
        stats = stats_ref[t, :, :]
        far_log = far_top + stats[1:2]
        top = jnp.maximum(stats[0:1], far_log)
        w_near, w_far = jnp.exp(stats[0:1] - top), jnp.exp(far_log - top)
        outs[t][...] = (w_far * far + w_near * nears[t][...]).astype(jnp.bfloat16)
        if t == 0:
            norm = w_far * far_norm + w_near * stats[2 : 2 + n]
            pad = jnp.zeros((state_ref.shape[0] - 1 - n, LANES), jnp.float32)
            state_ref[...] = jnp.concatenate([top, norm, pad], axis=0)


def inside_kernel(gates_ref, output_ref, queries_ref, keys_ref, values_ref, num_ref, cols_ref):
    rows = output_ref.shape[0]
    scale = queries_ref.shape[1] ** (-0.5)
    down = lax.broadcasted_iota(jnp.int32, (LANES, LANES), 0)
    across = lax.broadcasted_iota(jnp.int32, (LANES, LANES), 1)
    causal, same = down >= across, down == across
    lane = lax.broadcasted_iota(jnp.int32, (LANES, LANES), 1)
    gain = gates_ref[0:rows, :]
    cum_decay = gates_ref[rows : 2 * rows, :]
    open_gate = jax.nn.sigmoid(output_ref[...])

    def column(row):
        return jnp.sum(jnp.where(same, row, 0.0), axis=1, keepdims=True)

    before = jnp.full((1, 1), NEG, jnp.float32)
    for i in range(rows):
        here = slice(i * LANES, (i + 1) * LANES)
        a_row = gain[i : i + 1]
        peak = jnp.max(jnp.where(causal, a_row, NEG), axis=1, keepdims=True)
        peak = jnp.maximum(peak, before)
        before = jnp.maximum(before, jnp.max(a_row, axis=1, keepdims=True))
        width = (i + 1) * LANES
        scores = lax.dot_general(
            queries_ref[here, :],
            keys_ref[0:width, :],
            (((1,), (1,)), ((), ())),
            preferred_element_type=jnp.float32,
        )
        parts, den = [], 0.0
        for j in range(i + 1):
            diff = gain[j : j + 1] - peak
            if j == i:
                diff = jnp.where(causal, diff, NEG)
            part = jnp.exp(diff) * (scores[:, j * LANES : (j + 1) * LANES] * scale)
            den = den + part
            parts.append(part.astype(jnp.bfloat16))
        weighted = parts[0] if i == 0 else jnp.concatenate(parts, axis=1)
        den = jnp.sum(den, axis=1, keepdims=True)
        num_ref[here, :] = jnp.dot(
            weighted, values_ref[0:width, :], preferred_element_type=jnp.float32
        )
        cols = jnp.where(lane == 0, den, peak)
        cols = jnp.where(lane == 2, column(cum_decay[i : i + 1]), cols)
        cols_ref[here, :] = jnp.where(lane == 3, column(open_gate[i : i + 1]), cols)


def rescale_kernel(state_ref, queries_ref, num_ref, cols_ref, done_ref, lift_ref):
    width = queries_ref.shape[1]
    n = width // LANES
    scale = width ** (-0.5)
    top_prev = state_ref[0:1, 0:1]
    norm = jnp.concatenate([state_ref[1 + i : 2 + i, :] for i in range(n)], axis=1)
    for i in range(queries_ref.shape[0] // LANES):
        here = slice(i * LANES, (i + 1) * LANES)
        den_out = jnp.sum(queries_ref[here, :].astype(jnp.float32) * norm, axis=1, keepdims=True)
        cols = cols_ref[here, :]
        den_in, peak = cols[:, 0:1], cols[:, 1:2]
        cum_decay, open_gate = cols[:, 2:3], cols[:, 3:4]
        top = jnp.maximum(peak, top_prev)
        keep, lift = jnp.exp(peak - top), jnp.exp(top_prev - top) * scale
        den = jnp.abs(keep * den_in + lift * den_out)
        ratio = open_gate / jnp.maximum(den, jnp.exp(-(cum_decay + top)))
        done_ref[here, :] = (keep * ratio) * num_ref[here, :]
        lift_ref[here, :] = jnp.broadcast_to(lift * ratio, (LANES, LANES))


def output_kernel(inner, queries_ref, done_ref, lift_ref, *rest):
    pieces, out_ref, memory = rest[:inner], rest[inner], rest[inner + 1]
    member = lax.rem(lax.axis_index("ctx"), inner)
    piece = memory.shape[0] // inner
    for k in range(inner):
        start = pl.multiple_of(source(member, k, inner) * piece, piece)
        for i in range(memory.shape[1] // LANES):
            memory[pl.ds(start, piece), i * LANES : (i + 1) * LANES] = pieces[k][
                i * piece : (i + 1) * piece, :
            ]
    for i in range(queries_ref.shape[0] // LANES):
        here = slice(i * LANES, (i + 1) * LANES)
        num_out = jnp.dot(queries_ref[here, :], memory[...], preferred_element_type=jnp.float32)
        gated = done_ref[here, :] + lift_ref[here, 0:1] * num_out
        out_ref[here, :] = gated.astype(jnp.bfloat16)


def own_kernel(heads, orders, rows, gated_ref, *refs):
    bufs, (part_ref, other_ref, weights) = refs[:-3], refs[-3:]
    place, head = lax.axis_index("ctx"), lax.axis_index("head")
    at = 0
    for buf in bufs:
        for s in range(buf.shape[0] // rows):
            even, odd = (order[at] for order in orders)
            block = place ^ (even if even == odd else jnp.where(head % 2 == 0, even, odd))
            start = pl.multiple_of(block * rows, rows)
            weights[pl.ds(start, rows), :] = buf[s * rows : (s + 1) * rows, :]
            at += 1
    width = gated_ref.shape[1]
    for k in range(1, heads):
        start = pl.multiple_of(source(head, k, heads) * width, width)
        other_ref[(k - 1) * width : k * width, :] = weights[pl.ds(start, width), :]
    mine = weights[pl.ds(pl.multiple_of(head * width, width), width), :]
    part_ref[...] = jnp.dot(gated_ref[...], mine, preferred_element_type=jnp.float32)


def others_kernel(part_ref, other_ref, *refs):
    gated, out_ref = refs[:-1], refs[-1]
    total, at = part_ref[...], 0
    for g in gated:
        weights = other_ref[at : at + g.shape[1], :]
        total = total + jnp.dot(g[...], weights, preferred_element_type=jnp.float32)
        at += g.shape[1]
    out_ref[...] = total.astype(jnp.bfloat16)


def join_kernel(a_ref, b_ref, out_ref):
    rows = a_ref.shape[0]
    out_ref[0:rows, :] = a_ref[...]
    out_ref[rows:, :] = b_ref[...]


def call(kernel, out_shape, args, scratch=(), micros=1.0, after=(), plain=(), mib=24):
    skip = len(after)
    anywhere, vmem = pl.BlockSpec(memory_space=pl.ANY), pl.BlockSpec(memory_space=pltpu.VMEM)
    hbm = pl.BlockSpec(memory_space=pltpu.HBM)
    return pl.pallas_call(
        lambda *refs: kernel(*refs[skip:]),
        out_shape=out_shape,
        in_specs=[anywhere] * skip + [hbm if i in plain else vmem for i in range(len(args))],
        out_specs=jax.tree.map(lambda _: vmem, out_shape),
        scratch_shapes=scratch,
        compiler_params=pltpu.CompilerParams(vmem_limit_bytes=mib * 2**20),
        cost_estimate=pl.CostEstimate(
            flops=int(micros * 1.1e9), bytes_accessed=int(micros * 3.7e6), transcendentals=0
        ),
    )(*after, *args)


def shape(dims, dtype):
    return jax.ShapeDtypeStruct(dims, dtype)


def join(pair, after=()):
    rows, width = pair[0].shape
    return call(join_kernel, shape((2 * rows, width), pair[0].dtype), pair, micros=0.5, after=after)


def doubling_steps(n_ctx):
    assert is_pow2(n_ctx) and n_ctx >= 4
    return [1 << b for b in reversed(range(2, n_ctx.bit_length() - 1))]


def local(n_ctx, n_head, queries, keys, values, input_pre, forget_pre, output_pre, w_out):
    tok, width_k = queries.shape
    width_v = values.shape[1]
    inner, outer = split_groups(n_ctx)
    piece = width_k // inner
    bf16, f32 = jnp.bfloat16, jnp.float32
    gate_rows = tok // LANES
    forget, gate_in, gate_out = (
        g.reshape(gate_rows, LANES) for g in (forget_pre, input_pre, output_pre)
    )

    steps = doubling_steps(n_ctx)
    w_bufs, order = [w_out], [0]

    def trade(held, even, odd):
        pairs = [
            (j * n_head + h, (j ^ (odd if h % 2 else even)) * n_head + h)
            for j in range(n_ctx)
            for h in range(n_head)
        ]
        return lax.ppermute(held, ("ctx", "head"), pairs)

    def gather_step(after):
        held = join(w_bufs, after) if len(w_bufs) > 1 else w_bufs[0]
        if steps:
            step = steps.pop(0)
            w_bufs[:] = [held, trade(held, step, step)]
            order.extend([x ^ step for x in order])
        else:
            first, second = trade(held, 2, 1), trade(held, 1, 2)
            w_bufs[:] = [held, first, second, trade(first, 1, 2)]
        return [held]

    gather_step([])
    memory_rows = piece * width_v // LANES
    message = shape((memory_rows + rows_for(width_k), LANES), bf16)
    gates, *sends = call(
        functools.partial(summary_kernel, inner),
        [shape((2 * gate_rows, LANES), f32)] + [message] * inner,
        (forget, gate_in, keys, values),
        [
            pltpu.VMEM((width_k, width_v), f32),
            *[pltpu.VMEM(x.shape, x.dtype) for x in (forget, gate_in, keys, values)],
            pltpu.SemaphoreType.DMA((4,)),
        ],
        micros=2.0,
        plain=(0, 1, 2, 3),
        mib=60,
    )
    ready = gather_step([gates])
    blocks = [sends[0]] + [
        lax.ppermute(sends[k], "ctx", inner_pairs(n_ctx, inner, k)) for k in range(1, inner)
    ]
    num_in, cols = call(
        inside_kernel,
        [shape((tok, width_v), f32), shape((tok, LANES), f32)],
        (gates, gate_out, queries, keys, values),
        micros=8.0,
        after=ready,
    )
    total = call(functools.partial(group_total_kernel, inner, width_k), message, blocks)
    while steps:
        gather_step([total])
    ready = gather_step([total])
    totals = [
        lax.ppermute(total, "ctx", outer_pairs(n_ctx, inner, k)) for k in range(1, outer)
    ]
    *nears, stats = call(
        functools.partial(near_kernel, inner, width_k),
        [shape((memory_rows, LANES), f32)] * inner + [shape((inner, 8, LANES), f32)],
        blocks,
        micros=0.3,
        after=[*ready, cols],
    )
    *prefixes, state = call(
        functools.partial(far_kernel, inner, outer, width_k),
        [shape((memory_rows, LANES), bf16)] * inner + [shape((8, LANES), f32)],
        (stats, *totals, *nears),
        micros=0.1,
        after=w_bufs[1:2],
    )
    parts = [prefixes[0]] + [
        lax.ppermute(prefixes[k], "ctx", inner_pairs(n_ctx, inner, k)) for k in range(1, inner)
    ]
    done, lift = call(
        rescale_kernel,
        [shape((tok, width_v), f32), shape((tok, LANES), f32)],
        (state, queries, num_in, cols),
        micros=8.0,
        after=w_bufs[1:4],
    )
    gated = call(
        functools.partial(output_kernel, inner),
        shape((tok, width_v), bf16),
        (queries, done, lift, *parts),
        [pltpu.VMEM((width_k, width_v), bf16)],
        micros=0.1,
    )
    others = [
        lax.ppermute(gated, "head", [(j, target(j, k, n_head)) for j in range(n_head)])
        for k in range(1, n_head)
    ]
    cols_out = w_out.shape[1]
    w_orders = [[x ^ s for s in (0, a, b, a ^ b) for x in order] for a, b in ((2, 1), (1, 2))]
    part, other_rows = call(
        functools.partial(own_kernel, n_head, w_orders, w_out.shape[0]),
        [shape((tok, cols_out), f32), shape(((n_head - 1) * width_v, cols_out), bf16)],
        (gated, *w_bufs),
        [pltpu.VMEM((n_ctx * w_out.shape[0], cols_out), bf16)],
        micros=2.0,
    )
    return call(
        others_kernel, shape((tok, cols_out), bf16), (part, other_rows, *others), micros=1.0
    )


def solution(mesh):
    spec = P("ctx", "head")
    return jax.shard_map(
        functools.partial(local, mesh.shape["ctx"], mesh.shape["head"]),
        mesh=mesh,
        in_specs=(spec,) * 7,
        out_specs=spec,
        check_vma=False,
    )
```

```python
import functools

import jax
import jax.numpy as jnp
from jax import lax
from jax.experimental import pallas as pl
from jax.experimental.pallas import tpu as pltpu
from jax.sharding import PartitionSpec as P

TILE = 16
LANES = 128
NEG = -1e30


def split_groups(n):
    inner = max(a for a in range(1, n + 1) if n % a == 0 and a * a <= n)
    return inner, n // inner


def is_pow2(n):
    return n & (n - 1) == 0


def source(i, k, n):
    return i ^ k if is_pow2(n) else (i + k) % n


def target(i, k, n):
    return i ^ k if is_pow2(n) else (i + n - k) % n


def inner_pairs(n, inner, k):
    return [(j, j - j % inner + target(j % inner, k, inner)) for j in range(n)]


def outer_pairs(n, inner, k):
    outer = n // inner
    return [(j, target(j // inner, k, outer) * inner + j % inner) for j in range(n)]


def pieces3(x):
    hi = x.astype(jnp.bfloat16)
    rest = x - hi.astype(jnp.float32)
    mid = rest.astype(jnp.bfloat16)
    low = (rest - mid.astype(jnp.float32)).astype(jnp.bfloat16)
    return hi, mid, low


def lane_blocks(x):
    return [x[:, i : i + LANES] for i in range(0, x.shape[1], LANES)]


def rows_for(width_k):
    rows = 3 * (width_k // LANES + 2)
    return rows + -rows % TILE


def write_tail(ref, at, norm, top, decay):
    wide = jnp.concatenate([norm] + [jnp.broadcast_to(x, (1, LANES)) for x in (top, decay)], axis=0)
    rows = [p.astype(jnp.float32) for p in pieces3(wide)]
    count = ref.shape[0] - at - 3 * wide.shape[0]
    if count:
        rows.append(jnp.zeros((count, LANES), jnp.float32))
    ref[at:, :] = jnp.concatenate(rows, axis=0).astype(jnp.bfloat16)


def read_tail(ref, at, width_k):
    tail = ref[at:, :].astype(jnp.float32)
    n = width_k // LANES
    tail = tail[0 : n + 2] + tail[n + 2 : 2 * n + 4] + tail[2 * n + 4 : 3 * n + 6]
    return tail[0:n], tail[n : n + 1], tail[n + 1 : n + 2]


def read_tails(refs, width_k):
    at = refs[0].shape[0] - rows_for(width_k)
    return at, zip(*[read_tail(r, at, width_k) for r in refs])


def summary_kernel(inner, *refs):
    given, gates_ref, outs = refs[:4], refs[4], refs[5 : 5 + inner]
    memory, sems = refs[5 + inner], refs[-1]
    held = forget_ref, input_ref, keys_ref, values_ref = refs[6 + inner : -1]
    copies = [
        pltpu.make_async_copy(src, dst, sems.at[i]) for i, (src, dst) in enumerate(zip(given, held))
    ]
    for copy in copies:
        copy.start()
    copies[0].wait()
    copies[1].wait()
    member = lax.rem(lax.axis_index("ctx"), inner)
    rows = forget_ref.shape[0]
    forget = forget_ref[...]
    log_keep = jnp.minimum(forget, 0.0) - jnp.log1p(jnp.exp(-jnp.abs(forget)))
    tri = lax.broadcasted_iota(jnp.int32, (LANES, LANES), 0) <= lax.broadcasted_iota(
        jnp.int32, (LANES, LANES), 1
    )
    parts = jnp.concatenate([p.astype(jnp.float32) for p in pieces3(log_keep)], axis=0)
    sums = jnp.dot(
        parts.astype(jnp.bfloat16),
        tri.astype(jnp.bfloat16),
        preferred_element_type=jnp.float32,
    )
    inside = sums[:rows] + sums[rows : 2 * rows] + sums[2 * rows : 3 * rows]
    base = jnp.zeros((1, 1), jnp.float32)
    cum = []
    for r in range(rows):
        row = inside[r : r + 1]
        cum.append(row + base)
        base = base + row[:, LANES - 1 :]
    cum_decay = jnp.concatenate(cum, axis=0)
    gain = input_ref[...] - cum_decay
    top_gain = jnp.max(jnp.max(gain, axis=1, keepdims=True), axis=0, keepdims=True)
    weight = jnp.exp(gain - top_gain)
    gates_ref[0:rows, :] = gain
    gates_ref[rows : 2 * rows, :] = cum_decay
    along = jnp.concatenate([weight[r : r + 1] for r in range(rows)], axis=1)
    three = [p.astype(jnp.float32) for p in pieces3(along)]
    three.append(jnp.zeros((TILE - 3, along.shape[1]), jnp.float32))
    three = jnp.concatenate(three, axis=0).astype(jnp.bfloat16)
    copies[2].wait()
    keys = keys_ref[...]
    scaled = (keys.astype(jnp.float32).T * along).astype(jnp.bfloat16)
    norms = jnp.dot(three, keys, preferred_element_type=jnp.float32)
    norm = jnp.concatenate(lane_blocks(norms[0:1] + norms[1:2] + norms[2:3]), axis=0)
    copies[3].wait()
    memory[...] = jnp.dot(scaled, values_ref[...], preferred_element_type=jnp.float32)
    piece = memory.shape[0] // inner
    for k, out_ref in enumerate(outs):
        start = pl.multiple_of(target(member, k, inner) * piece, piece)
        wide = memory[pl.ds(start, piece), :].astype(jnp.bfloat16)
        for i, block in enumerate(lane_blocks(wide)):
            out_ref[i * piece : (i + 1) * piece, :] = block
        write_tail(out_ref, wide.size // LANES, norm, base + top_gain, base)


def chain_logs(where, tops, decays, end):
    logs = []
    for k in range(len(where)):
        log = tops[k]
        for o in range(len(where)):
            if o != k:
                between = jnp.logical_and(where[o] > where[k], where[o] < end)
                log = log + jnp.where(between, decays[o], 0.0)
        logs.append(jnp.where(where[k] < end, log, NEG))
    return logs


def chain_sum(where, logs, top, end, refs, at, norms):
    total, norm = 0.0, 0.0
    for k in range(len(where)):
        weight = jnp.where(where[k] < end, jnp.exp(logs[k] - top), 0.0)
        total = total + weight * refs[k][0:at, :].astype(jnp.float32)
        norm = norm + weight * norms[k]
    return total, norm


def group_total_kernel(inner, width_k, *refs):
    ins, out_ref = refs[:-1], refs[-1]
    member = lax.rem(lax.axis_index("ctx"), inner)
    where = [source(member, k, inner) for k in range(inner)]
    at, (norms, tops, decays) = read_tails(ins, width_k)
    logs = chain_logs(where, tops, decays, inner)
    top = functools.reduce(jnp.maximum, logs)
    total, norm = chain_sum(where, logs, top, inner, ins, at, norms)
    out_ref[0:at, :] = total.astype(jnp.bfloat16)
    write_tail(out_ref, at, norm, top, functools.reduce(jnp.add, decays))


def near_kernel(inner, width_k, *refs):
    ins, outs, stats_ref = refs[:inner], refs[inner:-1], refs[-1]
    member = lax.rem(lax.axis_index("ctx"), inner)
    where = [source(member, k, inner) for k in range(inner)]
    at, (norms, tops, decays) = read_tails(ins, width_k)
    for t in range(inner):
        end = target(member, t, inner)
        logs = chain_logs(where, tops, decays, end)
        top = functools.reduce(jnp.maximum, logs)
        total, norm = chain_sum(where, logs, top, end, ins, at, norms)
        outs[t][...] = total
        decay = 0.0
        for k in range(inner):
            decay = decay + jnp.where(where[k] < end, decays[k], 0.0)
        pad = jnp.zeros((8 - norm.shape[0] % 8 - 2, LANES), jnp.float32)
        stats_ref[t, :, :] = jnp.concatenate([top, decay, norm, pad], axis=0)


def far_kernel(inner, outer, width_k, stats_ref, *refs):
    totals, nears = refs[: outer - 1], refs[outer - 1 : outer - 1 + inner]
    outs, state_ref = refs[outer - 1 + inner : -1], refs[-1]
    group = lax.div(lax.axis_index("ctx"), inner)
    where = [source(group, k, outer) for k in range(1, outer)]
    at, (norms, tops, decays) = read_tails(totals, width_k)
    logs = chain_logs(where, tops, decays, group)
    far_top = functools.reduce(jnp.maximum, logs)
    far, far_norm = chain_sum(where, logs, far_top, group, totals, at, norms)
    n = width_k // LANES
    for t in range(inner):
        stats = stats_ref[t, :, :]
        far_log = far_top + stats[1:2]
        top = jnp.maximum(stats[0:1], far_log)
        w_near, w_far = jnp.exp(stats[0:1] - top), jnp.exp(far_log - top)
        outs[t][...] = (w_far * far + w_near * nears[t][...]).astype(jnp.bfloat16)
        if t == 0:
            norm = w_far * far_norm + w_near * stats[2 : 2 + n]
            pad = jnp.zeros((state_ref.shape[0] - 1 - n, LANES), jnp.float32)
            state_ref[...] = jnp.concatenate([top, norm, pad], axis=0)


def inside_kernel(gates_ref, output_ref, queries_ref, keys_ref, values_ref, num_ref, stats_ref):
    rows = queries_ref.shape[0] // LANES
    scale = queries_ref.shape[1] ** (-0.5)
    across = lax.broadcasted_iota(jnp.int32, (LANES, LANES), 1)
    causal = lax.broadcasted_iota(jnp.int32, (LANES, LANES), 0) >= across
    gain = gates_ref[0:rows, :]
    stats_ref[2 * rows : 3 * rows, :] = jax.nn.sigmoid(output_ref[...])
    before = jnp.full((1, 1), NEG, jnp.float32)
    for i in range(rows):
        here = slice(i * LANES, (i + 1) * LANES)
        a_row = gain[i : i + 1]
        peak = jnp.max(jnp.where(causal, a_row, NEG), axis=1, keepdims=True)
        peak = jnp.maximum(peak, before)
        before = jnp.maximum(before, jnp.max(a_row, axis=1, keepdims=True))
        width = (i + 1) * LANES
        scores = lax.dot_general(
            queries_ref[here, :],
            keys_ref[0:width, :],
            (((1,), (1,)), ((), ())),
            preferred_element_type=jnp.float32,
        )
        parts, den = [], 0.0
        for j in range(i + 1):
            diff = gain[j : j + 1] - peak
            if j == i:
                diff = jnp.where(causal, diff, NEG)
            part = jnp.exp(diff) * (scores[:, j * LANES : (j + 1) * LANES] * scale)
            den = den + part
            parts.append(part.astype(jnp.bfloat16))
        weighted = parts[0] if i == 0 else jnp.concatenate(parts, axis=1)
        den = jnp.sum(den, axis=1, keepdims=True)
        num_ref[here, :] = jnp.dot(
            weighted, values_ref[0:width, :], preferred_element_type=jnp.float32
        )
        turned = jnp.where(across == 0, den, peak).T
        stats_ref[i : i + 1, :] = turned[0:1]
        stats_ref[rows + i : rows + i + 1, :] = turned[1:2]


def rescale_kernel(state_ref, gates_ref, stats_ref, queries_ref, num_ref, done_ref, lift_ref):
    rows, width = gates_ref.shape[0] // 2, queries_ref.shape[1]
    n = width // LANES
    scale = width ** (-0.5)
    top_prev = state_ref[0:1, :]
    norm = jnp.concatenate([state_ref[1 + i : 2 + i, :] for i in range(n)], axis=1)
    three = [p.astype(jnp.float32) for p in pieces3(norm)]
    three.append(jnp.zeros((TILE - 3, width), jnp.float32))
    den_out = lax.dot_general(
        jnp.concatenate(three, axis=0).astype(jnp.bfloat16),
        queries_ref[...],
        (((1,), (1,)), ((), ())),
        preferred_element_type=jnp.float32,
    )
    den_out = jnp.concatenate(lane_blocks(den_out[0:1] + den_out[1:2] + den_out[2:3]), axis=0)
    den_in, peak = stats_ref[0:rows, :], stats_ref[rows : 2 * rows, :]
    top = jnp.maximum(peak, top_prev)
    keep, lift = jnp.exp(peak - top), jnp.exp(top_prev - top) * scale
    den = jnp.abs(keep * den_in + lift * den_out)
    floor = jnp.exp(-(gates_ref[rows : 2 * rows, :] + top))
    ratio = stats_ref[2 * rows : 3 * rows, :] / jnp.maximum(den, floor)
    keep, lift = keep * ratio, lift * ratio
    for i in range(rows):
        here = slice(i * LANES, (i + 1) * LANES)
        column = jnp.broadcast_to(keep[i : i + 1], (LANES, LANES)).T
        for j in range(num_ref.shape[1] // LANES):
            there = slice(j * LANES, (j + 1) * LANES)
            done_ref[here, there] = column * num_ref[here, there]
        lift_ref[here, :] = jnp.broadcast_to(lift[i : i + 1], (LANES, LANES)).T


def output_kernel(inner, queries_ref, done_ref, lift_ref, *rest):
    pieces, outs, memory = rest[:inner], rest[inner:-1], rest[-1]
    member = lax.rem(lax.axis_index("ctx"), inner)
    piece = memory.shape[0] // inner
    for k in range(inner):
        start = pl.multiple_of(source(member, k, inner) * piece, piece)
        for i in range(memory.shape[1] // LANES):
            memory[pl.ds(start, piece), i * LANES : (i + 1) * LANES] = pieces[k][
                i * piece : (i + 1) * piece, :
            ]
    rows = outs[0].shape[0]
    for i, out_ref in enumerate(outs):
        here = slice(i * rows, (i + 1) * rows)
        num_out = jnp.dot(queries_ref[here, :], memory[...], preferred_element_type=jnp.float32)
        column = lift_ref[here, :]
        for j, block in enumerate(lane_blocks(num_out)):
            there = slice(j * LANES, (j + 1) * LANES)
            out_ref[:, there] = (done_ref[here, there] + column * block).astype(jnp.bfloat16)


def project_kernel(heads, orders, rows, chunks, *refs):
    gated = [refs[k * chunks : (k + 1) * chunks] for k in range(heads)]
    bufs, (out_hbm, weights, held, sems) = refs[heads * chunks : -4], refs[-4:]
    place, head = lax.axis_index("ctx"), lax.axis_index("head")
    at = 0
    for buf in bufs:
        for s in range(buf.shape[0] // rows):
            even, odd = (order[at] for order in orders)
            block = place ^ (even if even == odd else jnp.where(head % 2 == 0, even, odd))
            start = pl.multiple_of(block * rows, rows)
            weights[pl.ds(start, rows), :] = buf[s * rows : (s + 1) * rows, :]
            at += 1
    tok, width = gated[0][0].shape
    copies = []
    for c in range(chunks):
        total = 0.0
        for k in range(heads):
            start = pl.multiple_of(source(head, k, heads) * width, width)
            part = weights[pl.ds(start, width), :]
            total = total + jnp.dot(gated[k][c][...], part, preferred_element_type=jnp.float32)
        held[c, :, :] = total.astype(jnp.bfloat16)
        to = out_hbm.at[pl.ds(c * tok, tok), :]
        copies.append(pltpu.make_async_copy(held.at[c], to, sems.at[c]))
        copies[-1].start()
    for copy in copies:
        copy.wait()


def join_kernel(*refs):
    out_ref, at = refs[-1], 0
    for ref in refs[:-1]:
        out_ref[at : at + ref.shape[0], :] = ref[...]
        at += ref.shape[0]


def call(kernel, out_shape, args, scratch=(), micros=1.0, after=(), plain=(), to_hbm=False):
    skip = len(after)
    anywhere, hbm, vmem = (
        pl.BlockSpec(memory_space=m) for m in (pl.ANY, pltpu.HBM, pltpu.VMEM)
    )
    return pl.pallas_call(
        lambda *refs: kernel(*refs[skip:]),
        out_shape=out_shape,
        in_specs=[anywhere] * skip + [hbm if i in plain else vmem for i in range(len(args))],
        out_specs=jax.tree.map(lambda _: hbm if to_hbm else vmem, out_shape),
        scratch_shapes=scratch,
        compiler_params=pltpu.CompilerParams(vmem_limit_bytes=24 * 2**20),
        cost_estimate=pl.CostEstimate(
            flops=int(micros * 1.1e9), bytes_accessed=int(micros * 3.7e6), transcendentals=0
        ),
    )(*after, *args)


def shape(dims, dtype):
    return jax.ShapeDtypeStruct(dims, dtype)


def join(parts, after=(), micros=0.5):
    out = shape((sum(p.shape[0] for p in parts), parts[0].shape[1]), parts[0].dtype)
    return call(join_kernel, out, parts, micros=micros, after=after)


def doubling_steps(n_ctx):
    assert is_pow2(n_ctx) and n_ctx >= 4
    return [1 << b for b in reversed(range(2, n_ctx.bit_length() - 1))]


def local(n_ctx, n_head, queries, keys, values, input_pre, forget_pre, output_pre, w_out):
    tok, width_k = queries.shape
    width_v = values.shape[1]
    inner, outer = split_groups(n_ctx)
    piece = width_k // inner
    bf16, f32 = jnp.bfloat16, jnp.float32
    gate_rows = tok // LANES
    forget, gate_in, gate_out = (
        g.reshape(gate_rows, LANES) for g in (forget_pre, input_pre, output_pre)
    )
    memory_rows = piece * width_v // LANES
    message = shape((memory_rows + rows_for(width_k), LANES), bf16)

    def over_ctx(held, even, odd):
        pairs = [
            (j * n_head + h, (j ^ (odd if h % 2 else even)) * n_head + h)
            for j in range(n_ctx)
            for h in range(n_head)
        ]
        return lax.ppermute(held, ("ctx", "head"), pairs)

    def in_group(sent):
        return sent[:1] + [
            lax.ppermute(sent[k], "ctx", inner_pairs(n_ctx, inner, k)) for k in range(1, inner)
        ]

    steps = doubling_steps(n_ctx)
    order = [0]
    w_parts = [w_out]

    def double(after):
        held = w_parts[0] if len(w_parts) == 1 else join(w_parts, after)
        if not steps:
            return held
        step = steps.pop(0)
        w_parts[:] = [held, over_ctx(held, step, step)]
        order.extend([x ^ step for x in order])
        return held

    double([])
    gates, *sends = call(
        functools.partial(summary_kernel, inner),
        [shape((2 * gate_rows, LANES), f32)] + [message] * inner,
        [
            pltpu.with_memory_space_constraint(x, pltpu.HBM)
            for x in (forget, gate_in, keys, values)
        ],
        [
            pltpu.VMEM((width_k, width_v), f32),
            *[pltpu.VMEM(x.shape, x.dtype) for x in (forget, gate_in, keys, values)],
            pltpu.SemaphoreType.DMA((4,)),
        ],
        micros=2.0,
        plain=(0, 1, 2, 3),
    )
    blocks = in_group(sends)
    held = double([gates])
    num_in, stats_in = call(
        inside_kernel,
        [shape((tok, width_v), f32), shape((3 * gate_rows, LANES), f32)],
        (gates, gate_out, queries, keys, values),
        micros=8.0,
        after=[held],
    )
    total = call(
        functools.partial(group_total_kernel, inner, width_k), message, blocks, after=[stats_in]
    )
    totals = [
        lax.ppermute(total, "ctx", outer_pairs(n_ctx, inner, k)) for k in range(1, outer)
    ]
    while steps:
        double([total])
    held = double([total])

    one, other = (1, 2), (2, 1)
    first = over_ctx(held, *one)
    *nears, stats = call(
        functools.partial(near_kernel, inner, width_k),
        [shape((memory_rows, LANES), f32)] * inner + [shape((inner, 8, LANES), f32)],
        blocks,
        micros=8.0,
        after=[held, stats_in],
    )
    again = join([held], [stats])
    second, third = over_ctx(again, *other), over_ctx(first, *other)
    orders = [[x ^ s for s in (0, a, b, a ^ b) for x in order] for a, b in zip(one, other)]
    *prefixes, state = call(
        functools.partial(far_kernel, inner, outer, width_k),
        [shape((memory_rows, LANES), bf16)] * inner + [shape((8, LANES), f32)],
        (stats, *totals, *nears),
        micros=8.0,
    )
    parts = in_group(prefixes)
    done, lift = call(
        rescale_kernel,
        [shape((tok, width_v), f32), shape((tok, LANES), f32)],
        (state, gates, stats_in, queries, num_in),
        micros=8.0,
        after=[first, second],
    )
    chunks = tok // LANES
    gated = call(
        functools.partial(output_kernel, inner),
        [shape((LANES, width_v), bf16)] * chunks,
        (queries, done, lift, *parts),
        [pltpu.VMEM((width_k, width_v), bf16)],
        micros=0.1,
    )
    others = [
        lax.ppermute(g, "head", [(j, target(j, k, n_head)) for j in range(n_head)])
        for k in range(1, n_head)
        for g in gated
    ]
    return call(
        functools.partial(project_kernel, n_head, orders, w_out.shape[0], chunks),
        shape((tok, w_out.shape[1]), bf16),
        (*gated, *others, held, first, second, third),
        [
            pltpu.VMEM((n_ctx * w_out.shape[0], w_out.shape[1]), bf16),
            pltpu.VMEM((chunks, LANES, w_out.shape[1]), bf16),
            pltpu.SemaphoreType.DMA((chunks,)),
        ],
        micros=1.0,
        to_hbm=True,
    )


def solution(mesh):
    spec = P("ctx", "head")
    return jax.shard_map(
        functools.partial(local, mesh.shape["ctx"], mesh.shape["head"]),
        mesh=mesh,
        in_specs=(spec,) * 7,
        out_specs=spec,
        check_vma=False,
    )
```

```python
import functools

import jax
import jax.numpy as jnp
from jax import lax
from jax.experimental import pallas as pl
from jax.experimental.pallas import tpu as pltpu
from jax.sharding import PartitionSpec as P

TILE = 16
LANES = 128
NEG = -1e30


def split_groups(n):
    inner = max(a for a in range(1, n + 1) if n % a == 0 and a * a <= n)
    return inner, n // inner


def is_pow2(n):
    return n & (n - 1) == 0


def source(i, k, n):
    return i ^ (-k % n) if is_pow2(n) else (i + k) % n


def target(i, k, n):
    return i ^ (-k % n) if is_pow2(n) else (i + n - k) % n


def exchange(i, j, n):
    return lax.rem(n - (i ^ j) if is_pow2(n) else j + n - i, n)


def inner_pairs(n, inner, k):
    return [(j, j - j % inner + target(j % inner, k, inner)) for j in range(n)]


def far_order(outer):
    order = list(range(1, outer))
    return order[1::-1] + order[2:]


def outer_pairs(n, inner, k):
    outer = n // inner
    return [(j, target(j // inner, k, outer) * inner + j % inner) for j in range(n)]


def pieces3(x):
    hi = x.astype(jnp.bfloat16)
    rest = x - hi.astype(jnp.float32)
    mid = rest.astype(jnp.bfloat16)
    low = (rest - mid.astype(jnp.float32)).astype(jnp.bfloat16)
    return hi, mid, low


def lane_blocks(x):
    return [x[:, i : i + LANES] for i in range(0, x.shape[1], LANES)]


def rows_for(width_k):
    rows = 3 * (width_k // LANES + 2)
    return rows + -rows % TILE


def write_tail(ref, at, norm, top, decay):
    wide = jnp.concatenate([norm] + [jnp.broadcast_to(x, (1, LANES)) for x in (top, decay)], axis=0)
    rows = [p.astype(jnp.float32) for p in pieces3(wide)]
    count = ref.shape[0] - at - 3 * wide.shape[0]
    if count:
        rows.append(jnp.zeros((count, LANES), jnp.float32))
    ref[at:, :] = jnp.concatenate(rows, axis=0).astype(jnp.bfloat16)


def read_tail(ref, at, width_k):
    tail = ref[at:, :].astype(jnp.float32)
    n = width_k // LANES
    tail = tail[0 : n + 2] + tail[n + 2 : 2 * n + 4] + tail[2 * n + 4 : 3 * n + 6]
    return tail[0:n], tail[n : n + 1], tail[n + 1 : n + 2]


def read_tails(refs, width_k):
    at = refs[0].shape[0] - rows_for(width_k)
    return at, zip(*[read_tail(r, at, width_k) for r in refs])


def summary_kernel(inner, *refs):
    given, gates_ref, outs = refs[:4], refs[4], refs[5 : 5 + inner]
    memory, sems = refs[5 + inner], refs[-1]
    held = forget_ref, input_ref, keys_ref, values_ref = refs[6 + inner : -1]
    copies = [
        pltpu.make_async_copy(src, dst, sems.at[i]) for i, (src, dst) in enumerate(zip(given, held))
    ]
    for copy in copies:
        copy.start()
    copies[0].wait()
    copies[1].wait()
    member = lax.rem(lax.axis_index("ctx"), inner)
    rows = forget_ref.shape[0]
    forget = forget_ref[...]
    log_keep = jnp.minimum(forget, 0.0) - jnp.log1p(jnp.exp(-jnp.abs(forget)))
    tri = lax.broadcasted_iota(jnp.int32, (LANES, LANES), 0) <= lax.broadcasted_iota(
        jnp.int32, (LANES, LANES), 1
    )
    parts = jnp.concatenate([p.astype(jnp.float32) for p in pieces3(log_keep)], axis=0)
    sums = jnp.dot(
        parts.astype(jnp.bfloat16),
        tri.astype(jnp.bfloat16),
        preferred_element_type=jnp.float32,
    )
    inside = sums[:rows] + sums[rows : 2 * rows] + sums[2 * rows : 3 * rows]
    base = jnp.zeros((1, 1), jnp.float32)
    cum = []
    for r in range(rows):
        row = inside[r : r + 1]
        cum.append(row + base)
        base = base + row[:, LANES - 1 :]
    cum_decay = jnp.concatenate(cum, axis=0)
    gain = input_ref[...] - cum_decay
    top_gain = jnp.max(jnp.max(gain, axis=1, keepdims=True), axis=0, keepdims=True)
    weight = jnp.exp(gain - top_gain)
    gates_ref[0:rows, :] = gain
    gates_ref[rows : 2 * rows, :] = cum_decay
    along = jnp.concatenate([weight[r : r + 1] for r in range(rows)], axis=1)
    three = [p.astype(jnp.float32) for p in pieces3(along)]
    three.append(jnp.zeros((TILE - 3, along.shape[1]), jnp.float32))
    three = jnp.concatenate(three, axis=0).astype(jnp.bfloat16)
    copies[2].wait()
    keys = keys_ref[...]
    scaled = (keys.astype(jnp.float32).T * along).astype(jnp.bfloat16)
    norms = jnp.dot(three, keys, preferred_element_type=jnp.float32)
    norm = jnp.concatenate(lane_blocks(norms[0:1] + norms[1:2] + norms[2:3]), axis=0)
    copies[3].wait()
    memory[...] = jnp.dot(scaled, values_ref[...], preferred_element_type=jnp.float32)
    piece = memory.shape[0] // inner
    for k, out_ref in enumerate(outs):
        start = pl.multiple_of(target(member, k, inner) * piece, piece)
        wide = memory[pl.ds(start, piece), :].astype(jnp.bfloat16)
        for i, block in enumerate(lane_blocks(wide)):
            out_ref[i * piece : (i + 1) * piece, :] = block
        write_tail(out_ref, wide.size // LANES, norm, base + top_gain, base)


def chain_logs(where, tops, decays, end):
    logs = []
    for k in range(len(where)):
        log = tops[k]
        for o in range(len(where)):
            if o != k:
                between = jnp.logical_and(where[o] > where[k], where[o] < end)
                log = log + jnp.where(between, decays[o], 0.0)
        logs.append(jnp.where(where[k] < end, log, NEG))
    return logs


def chain_sum(where, logs, top, end, refs, at, norms):
    total, norm = 0.0, 0.0
    for k in range(len(where)):
        weight = jnp.where(where[k] < end, jnp.exp(logs[k] - top), 0.0)
        total = total + weight * refs[k][0:at, :].astype(jnp.float32)
        norm = norm + weight * norms[k]
    return total, norm


def group_total_kernel(inner, width_k, *refs):
    ins, out_ref = refs[:-1], refs[-1]
    member = lax.rem(lax.axis_index("ctx"), inner)
    where = [source(member, k, inner) for k in range(inner)]
    at, (norms, tops, decays) = read_tails(ins, width_k)
    logs = chain_logs(where, tops, decays, inner)
    top = functools.reduce(jnp.maximum, logs)
    total, norm = chain_sum(where, logs, top, inner, ins, at, norms)
    out_ref[0:at, :] = total.astype(jnp.bfloat16)
    write_tail(out_ref, at, norm, top, functools.reduce(jnp.add, decays))


def near_kernel(inner, width_k, *refs):
    ins, outs, stats_ref = refs[:inner], refs[inner:-1], refs[-1]
    member = lax.rem(lax.axis_index("ctx"), inner)
    where = [source(member, k, inner) for k in range(inner)]
    at, (norms, tops, decays) = read_tails(ins, width_k)
    for t in range(inner):
        end = target(member, t, inner)
        logs = chain_logs(where, tops, decays, end)
        top = functools.reduce(jnp.maximum, logs)
        total, norm = chain_sum(where, logs, top, end, ins, at, norms)
        outs[t][...] = total
        decay = 0.0
        for k in range(inner):
            decay = decay + jnp.where(where[k] < end, decays[k], 0.0)
        pad = jnp.zeros((8 - norm.shape[0] % 8 - 2, LANES), jnp.float32)
        stats_ref[t, :, :] = jnp.concatenate([top, decay, norm, pad], axis=0)


def far_kernel(inner, outer, width_k, stats_ref, *refs):
    totals, nears = refs[: outer - 1], refs[outer - 1 : outer - 1 + inner]
    outs, state_ref = refs[outer - 1 + inner : -1], refs[-1]
    group = lax.div(lax.axis_index("ctx"), inner)
    where = [source(group, k, outer) for k in far_order(outer)]
    at, (norms, tops, decays) = read_tails(totals, width_k)
    logs = chain_logs(where, tops, decays, group)
    far_top = functools.reduce(jnp.maximum, logs)
    far, far_norm = chain_sum(where, logs, far_top, group, totals, at, norms)
    n = width_k // LANES
    for t in range(inner):
        stats = stats_ref[t, :, :]
        far_log = far_top + stats[1:2]
        top = jnp.maximum(stats[0:1], far_log)
        w_near, w_far = jnp.exp(stats[0:1] - top), jnp.exp(far_log - top)
        outs[t][...] = (w_far * far + w_near * nears[t][...]).astype(jnp.bfloat16)
        if t == 0:
            norm = w_far * far_norm + w_near * stats[2 : 2 + n]
            pad = jnp.zeros((state_ref.shape[0] - 1 - n, LANES), jnp.float32)
            state_ref[...] = jnp.concatenate([top, norm, pad], axis=0)


def inside_kernel(gates_ref, output_ref, queries_ref, keys_ref, values_ref, num_ref, stats_ref):
    rows = queries_ref.shape[0] // LANES
    scale = queries_ref.shape[1] ** (-0.5)
    across = lax.broadcasted_iota(jnp.int32, (LANES, LANES), 1)
    causal = lax.broadcasted_iota(jnp.int32, (LANES, LANES), 0) >= across
    gain = gates_ref[0:rows, :]
    stats_ref[2 * rows : 3 * rows, :] = jax.nn.sigmoid(output_ref[...])
    before = jnp.full((1, 1), NEG, jnp.float32)
    for i in range(rows):
        here = slice(i * LANES, (i + 1) * LANES)
        a_row = gain[i : i + 1]
        peak = jnp.max(jnp.where(causal, a_row, NEG), axis=1, keepdims=True)
        peak = jnp.maximum(peak, before)
        before = jnp.maximum(before, jnp.max(a_row, axis=1, keepdims=True))
        width = (i + 1) * LANES
        scores = lax.dot_general(
            queries_ref[here, :],
            keys_ref[0:width, :],
            (((1,), (1,)), ((), ())),
            preferred_element_type=jnp.float32,
        )
        parts, den = [], 0.0
        for j in range(i + 1):
            diff = gain[j : j + 1] - peak
            if j == i:
                diff = jnp.where(causal, diff, NEG)
            part = jnp.exp(diff) * (scores[:, j * LANES : (j + 1) * LANES] * scale)
            den = den + part
            parts.append(part.astype(jnp.bfloat16))
        weighted = parts[0] if i == 0 else jnp.concatenate(parts, axis=1)
        den = jnp.sum(den, axis=1, keepdims=True)
        num_ref[here, :] = jnp.dot(
            weighted, values_ref[0:width, :], preferred_element_type=jnp.float32
        )
        turned = jnp.where(across == 0, den, peak).T
        stats_ref[i : i + 1, :] = turned[0:1]
        stats_ref[rows + i : rows + i + 1, :] = turned[1:2]


def rescale_kernel(state_ref, gates_ref, stats_ref, queries_ref, num_ref, done_ref, lift_ref):
    rows, width = gates_ref.shape[0] // 2, queries_ref.shape[1]
    n = width // LANES
    scale = width ** (-0.5)
    top_prev = state_ref[0:1, :]
    norm = jnp.concatenate([state_ref[1 + i : 2 + i, :] for i in range(n)], axis=1)
    three = [p.astype(jnp.float32) for p in pieces3(norm)]
    three.append(jnp.zeros((TILE - 3, width), jnp.float32))
    den_out = lax.dot_general(
        jnp.concatenate(three, axis=0).astype(jnp.bfloat16),
        queries_ref[...],
        (((1,), (1,)), ((), ())),
        preferred_element_type=jnp.float32,
    )
    den_out = jnp.concatenate(lane_blocks(den_out[0:1] + den_out[1:2] + den_out[2:3]), axis=0)
    den_in, peak = stats_ref[0:rows, :], stats_ref[rows : 2 * rows, :]
    top = jnp.maximum(peak, top_prev)
    keep, lift = jnp.exp(peak - top), jnp.exp(top_prev - top) * scale
    den = jnp.abs(keep * den_in + lift * den_out)
    floor = jnp.exp(-(gates_ref[rows : 2 * rows, :] + top))
    ratio = stats_ref[2 * rows : 3 * rows, :] / jnp.maximum(den, floor)
    keep, lift = keep * ratio, lift * ratio
    for i in range(rows):
        here = slice(i * LANES, (i + 1) * LANES)
        column = jnp.broadcast_to(keep[i : i + 1], (LANES, LANES)).T
        for j in range(num_ref.shape[1] // LANES):
            there = slice(j * LANES, (j + 1) * LANES)
            done_ref[here, there] = column * num_ref[here, there]
        lift_ref[here, :] = jnp.broadcast_to(lift[i : i + 1], (LANES, LANES)).T


def output_kernel(inner, queries_ref, done_ref, lift_ref, *rest):
    pieces, (out_ref, memory) = rest[:inner], rest[inner:]
    member = lax.rem(lax.axis_index("ctx"), inner)
    piece = memory.shape[0] // inner
    for k in range(inner):
        start = pl.multiple_of(source(member, k, inner) * piece, piece)
        for i in range(memory.shape[1] // LANES):
            memory[pl.ds(start, piece), i * LANES : (i + 1) * LANES] = pieces[k][
                i * piece : (i + 1) * piece, :
            ]
    for i in range(queries_ref.shape[0] // LANES):
        here = slice(i * LANES, (i + 1) * LANES)
        num_out = jnp.dot(queries_ref[here, :], memory[...], preferred_element_type=jnp.float32)
        column = lift_ref[here, :]
        for j, block in enumerate(lane_blocks(num_out)):
            there = slice(j * LANES, (j + 1) * LANES)
            out_ref[here, there] = (done_ref[here, there] + column * block).astype(jnp.bfloat16)


def own_kernel(heads, orders, rows, gated_ref, *refs):
    bufs, (part_ref, other_ref, mine) = refs[:-3], refs[-3:]
    place, head = lax.axis_index("ctx"), lax.axis_index("head")
    width = mine.shape[0]
    each = width // rows
    at = 0
    for buf in bufs:
        for s in range(buf.shape[0] // rows):
            even, odd = (order[at] for order in orders)
            block = place ^ (even if even == odd else jnp.where(head % 2 == 0, even, odd))
            owner, start = lax.div(block, each), pl.multiple_of(lax.rem(block, each) * rows, rows)
            here = buf.at[s * rows : (s + 1) * rows, :]

            @pl.when(owner == head)
            def _():
                mine[pl.ds(start, rows), :] = here[...]

            @pl.when(owner != head)
            def _():
                away = (exchange(head, owner, heads) - 1) * width + start
                other_ref[pl.ds(pl.multiple_of(away, rows), rows), :] = here[...]

            at += 1
    part_ref[...] = jnp.dot(gated_ref[...], mine[...], preferred_element_type=jnp.float32)


def others_kernel(part_ref, other_ref, *refs):
    gated, (out_hbm, held, sems) = refs[:-3], refs[-3:]
    width = gated[0].shape[1]
    steps, rows = held.shape[:2]
    copies = []
    for c in range(steps):
        here = slice(c * rows, (c + 1) * rows)
        total = part_ref[here, :]
        for k, g in enumerate(gated):
            part = other_ref[k * width : (k + 1) * width, :]
            total = total + jnp.dot(g[here, :], part, preferred_element_type=jnp.float32)
        held[c, :, :] = total.astype(jnp.bfloat16)
        copies.append(
            pltpu.make_async_copy(held.at[c], out_hbm.at[pl.ds(c * rows, rows), :], sems.at[c])
        )
        copies[-1].start()
    for copy in copies:
        copy.wait()


def join_kernel(*refs):
    out_ref, at = refs[-1], 0
    for ref in refs[:-1]:
        out_ref[at : at + ref.shape[0], :] = ref[...]
        at += ref.shape[0]


def call(kernel, out_shape, args, scratch=(), micros=1.0, after=(), plain=(), to_hbm=False):
    skip = len(after)
    anywhere, hbm, vmem = (
        pl.BlockSpec(memory_space=m) for m in (pl.ANY, pltpu.HBM, pltpu.VMEM)
    )
    return pl.pallas_call(
        lambda *refs: kernel(*refs[skip:]),
        out_shape=out_shape,
        in_specs=[anywhere] * skip + [hbm if i in plain else vmem for i in range(len(args))],
        out_specs=jax.tree.map(lambda _: hbm if to_hbm else vmem, out_shape),
        scratch_shapes=scratch,
        compiler_params=pltpu.CompilerParams(vmem_limit_bytes=24 * 2**20),
        cost_estimate=pl.CostEstimate(
            flops=int(micros * 1.1e9), bytes_accessed=int(micros * 3.7e6), transcendentals=0
        ),
    )(*after, *args)


def shape(dims, dtype):
    return jax.ShapeDtypeStruct(dims, dtype)


def join(parts, after=(), micros=0.5):
    out = shape((sum(p.shape[0] for p in parts), parts[0].shape[1]), parts[0].dtype)
    return call(join_kernel, out, parts, micros=micros, after=after)


def doubling_steps(n_ctx):
    assert is_pow2(n_ctx) and n_ctx >= 16
    return [1 << b for b in reversed(range(2, n_ctx.bit_length() - 1))]


def local(n_ctx, n_head, queries, keys, values, input_pre, forget_pre, output_pre, w_out):
    tok, width_k = queries.shape
    width_v = values.shape[1]
    inner, outer = split_groups(n_ctx)
    piece = width_k // inner
    bf16, f32 = jnp.bfloat16, jnp.float32
    gate_rows = tok // LANES
    forget, gate_in, gate_out = (
        g.reshape(gate_rows, LANES) for g in (forget_pre, input_pre, output_pre)
    )
    memory_rows = piece * width_v // LANES
    message = shape((memory_rows + rows_for(width_k), LANES), bf16)

    def over_ctx(held, even, odd):
        pairs = [
            (j * n_head + h, (j ^ (odd if h % 2 else even)) * n_head + h)
            for j in range(n_ctx)
            for h in range(n_head)
        ]
        return lax.ppermute(held, ("ctx", "head"), pairs)

    def in_group(sent):
        return sent[:1] + [
            lax.ppermute(sent[k], "ctx", inner_pairs(n_ctx, inner, k)) for k in range(1, inner)
        ]

    *steps, last = doubling_steps(n_ctx)
    order, halves = [0], [w_out]
    for step in steps:
        held = halves[0] if len(halves) == 1 else join(halves)
        halves = [held, over_ctx(held, step, step)]
        order.extend([x ^ step for x in order])

    gates, *sends = call(
        functools.partial(summary_kernel, inner),
        [shape((2 * gate_rows, LANES), f32)] + [message] * inner,
        [
            pltpu.with_memory_space_constraint(x, pltpu.HBM)
            for x in (forget, gate_in, keys, values)
        ],
        [
            pltpu.VMEM((width_k, width_v), f32),
            *[pltpu.VMEM(x.shape, x.dtype) for x in (forget, gate_in, keys, values)],
            pltpu.SemaphoreType.DMA((4,)),
        ],
        micros=2.0,
        plain=(0, 1, 2, 3),
    )
    blocks = in_group(sends)

    one, other = (1, 2), (2, 1)
    early = join(halves, [gates])
    late = over_ctx(early, last, last)
    first_early = over_ctx(early, *one)
    waited = join([gates], [early], 8.0)
    total = call(
        functools.partial(group_total_kernel, inner, width_k), message, blocks, after=[waited]
    )
    totals = [
        lax.ppermute(total, "ctx", outer_pairs(n_ctx, inner, k)) for k in far_order(outer)
    ]
    late = join([late], [total])
    first_late = over_ctx(late, *one)
    *nears, stats = call(
        functools.partial(near_kernel, inner, width_k),
        [shape((memory_rows, LANES), f32)] * inner + [shape((inner, 8, LANES), f32)],
        blocks,
        micros=8.0,
        after=[late],
    )
    held = join([early, late], [stats])
    second = over_ctx(held, *other)
    third_early = over_ctx(join([first_early], [stats]), *other)
    third_late = over_ctx(first_late, *other)
    orders = []
    for a, b in zip(one, other):
        halves = [order, [x ^ last for x in order]]
        orders.append(
            [x ^ s for s in (0, b) for half in halves for x in half]
            + [x ^ s for half in halves for s in (a, a ^ b) for x in half]
        )

    *prefixes, state = call(
        functools.partial(far_kernel, inner, outer, width_k),
        [shape((memory_rows, LANES), bf16)] * inner + [shape((8, LANES), f32)],
        (stats, *totals, *nears),
        micros=8.0,
        after=[held],
    )
    parts = in_group(prefixes)
    num_in, stats_in = call(
        inside_kernel,
        [shape((tok, width_v), f32), shape((3 * gate_rows, LANES), f32)],
        (gates, gate_out, queries, keys, values),
        micros=8.0,
        after=[state, third_early],
    )
    done, lift = call(
        rescale_kernel,
        [shape((tok, width_v), f32), shape((tok, LANES), f32)],
        (state, gates, stats_in, queries, num_in),
        micros=8.0,
        after=[first_late, third_early],
    )
    gated = call(
        functools.partial(output_kernel, inner),
        shape((tok, width_v), bf16),
        (queries, done, lift, *parts),
        [pltpu.VMEM((width_k, width_v), bf16)],
        micros=0.1,
        after=[second],
    )
    others = [
        lax.ppermute(gated, "head", [(j, target(j, k, n_head)) for j in range(n_head)])
        for k in range(1, n_head)
    ]
    cols_out = w_out.shape[1]
    part, other_rows = call(
        functools.partial(own_kernel, n_head, orders, w_out.shape[0]),
        [shape((tok, cols_out), f32), shape(((n_head - 1) * width_v, cols_out), bf16)],
        (gated, held, second, first_early, third_early, first_late, third_late),
        [pltpu.VMEM((width_v, cols_out), bf16)],
        micros=5.0,
    )
    return call(
        others_kernel,
        shape((tok, cols_out), bf16),
        (part, other_rows, *others),
        [
            pltpu.VMEM((gate_rows, LANES, cols_out), bf16),
            pltpu.SemaphoreType.DMA((gate_rows,)),
        ],
        micros=1.0,
        to_hbm=True,
    )


def solution(mesh):
    spec = P("ctx", "head")
    return jax.shard_map(
        functools.partial(local, mesh.shape["ctx"], mesh.shape["head"]),
        mesh=mesh,
        in_specs=(spec,) * 7,
        out_specs=spec,
        check_vma=False,
    )
```

```python
import functools

import jax
import jax.numpy as jnp
from jax import lax
from jax.experimental import pallas as pl
from jax.experimental.pallas import tpu as pltpu
from jax.sharding import PartitionSpec as P

TILE = 16
LANES = 128
NEG = -1e30


def split_groups(n):
    inner = max(a for a in range(1, n + 1) if n % a == 0 and a * a <= n)
    return inner, n // inner


def is_pow2(n):
    return n & (n - 1) == 0


def source(i, k, n):
    return i ^ (-k % n) if is_pow2(n) else (i + k) % n


def target(i, k, n):
    return i ^ (-k % n) if is_pow2(n) else (i + n - k) % n


def exchange(i, j, n):
    return lax.rem(n - (i ^ j) if is_pow2(n) else j + n - i, n)


def inner_pairs(n, inner, k):
    return [(j, j - j % inner + target(j % inner, k, inner)) for j in range(n)]


def far_order(outer):
    order = list(range(1, outer))
    return order[1::-1] + order[2:]


def outer_pairs(n, inner, k):
    outer = n // inner
    return [(j, target(j // inner, k, outer) * inner + j % inner) for j in range(n)]


def pieces3(x):
    hi = x.astype(jnp.bfloat16)
    rest = x - hi.astype(jnp.float32)
    mid = rest.astype(jnp.bfloat16)
    low = (rest - mid.astype(jnp.float32)).astype(jnp.bfloat16)
    return hi, mid, low


def lane_blocks(x):
    return [x[:, i : i + LANES] for i in range(0, x.shape[1], LANES)]


def rows_for(width_k):
    rows = 3 * (width_k // LANES + 2)
    return rows + -rows % TILE


def write_tail(ref, at, norm, top, decay):
    wide = jnp.concatenate([norm] + [jnp.broadcast_to(x, (1, LANES)) for x in (top, decay)], axis=0)
    rows = [p.astype(jnp.float32) for p in pieces3(wide)]
    count = ref.shape[0] - at - 3 * wide.shape[0]
    if count:
        rows.append(jnp.zeros((count, LANES), jnp.float32))
    ref[at:, :] = jnp.concatenate(rows, axis=0).astype(jnp.bfloat16)


def read_tail(ref, at, width_k):
    tail = ref[at:, :].astype(jnp.float32)
    n = width_k // LANES
    tail = tail[0 : n + 2] + tail[n + 2 : 2 * n + 4] + tail[2 * n + 4 : 3 * n + 6]
    return tail[0:n], tail[n : n + 1], tail[n + 1 : n + 2]


def read_tails(refs, width_k):
    at = refs[0].shape[0] - rows_for(width_k)
    return at, zip(*[read_tail(r, at, width_k) for r in refs])


def summary_kernel(inner, *refs):
    given, gates_ref, outs = refs[:4], refs[4], refs[5 : 5 + inner]
    memory, sems = refs[5 + inner], refs[-1]
    held = forget_ref, input_ref, keys_ref, values_ref = refs[6 + inner : -1]
    copies = [
        pltpu.make_async_copy(src, dst, sems.at[i]) for i, (src, dst) in enumerate(zip(given, held))
    ]
    for copy in copies:
        copy.start()
    copies[0].wait()
    copies[1].wait()
    member = lax.rem(lax.axis_index("ctx"), inner)
    rows = forget_ref.shape[0]
    forget = forget_ref[...]
    log_keep = jnp.minimum(forget, 0.0) - jnp.log1p(jnp.exp(-jnp.abs(forget)))
    tri = lax.broadcasted_iota(jnp.int32, (LANES, LANES), 0) <= lax.broadcasted_iota(
        jnp.int32, (LANES, LANES), 1
    )
    parts = jnp.concatenate([p.astype(jnp.float32) for p in pieces3(log_keep)], axis=0)
    sums = jnp.dot(
        parts.astype(jnp.bfloat16),
        tri.astype(jnp.bfloat16),
        preferred_element_type=jnp.float32,
    )
    inside = sums[:rows] + sums[rows : 2 * rows] + sums[2 * rows : 3 * rows]
    base = jnp.zeros((1, 1), jnp.float32)
    cum = []
    for r in range(rows):
        row = inside[r : r + 1]
        cum.append(row + base)
        base = base + row[:, LANES - 1 :]
    cum_decay = jnp.concatenate(cum, axis=0)
    gain = input_ref[...] - cum_decay
    top_gain = jnp.max(jnp.max(gain, axis=1, keepdims=True), axis=0, keepdims=True)
    weight = jnp.exp(gain - top_gain)
    gates_ref[0:rows, :] = gain
    gates_ref[rows : 2 * rows, :] = cum_decay
    along = jnp.concatenate([weight[r : r + 1] for r in range(rows)], axis=1)
    three = [p.astype(jnp.float32) for p in pieces3(along)]
    three.append(jnp.zeros((TILE - 3, along.shape[1]), jnp.float32))
    three = jnp.concatenate(three, axis=0).astype(jnp.bfloat16)
    copies[2].wait()
    keys = keys_ref[...]
    scaled = (keys.astype(jnp.float32).T * along).astype(jnp.bfloat16)
    norms = jnp.dot(three, keys, preferred_element_type=jnp.float32)
    norm = jnp.concatenate(lane_blocks(norms[0:1] + norms[1:2] + norms[2:3]), axis=0)
    copies[3].wait()
    whole = jnp.dot(scaled, values_ref[...], preferred_element_type=jnp.float32)
    memory[...] = whole.astype(jnp.bfloat16)
    piece = memory.shape[0] // inner
    for k, out_ref in enumerate(outs):
        start = pl.multiple_of(target(member, k, inner) * piece, piece)
        wide = memory[pl.ds(start, piece), :]
        for i, block in enumerate(lane_blocks(wide)):
            out_ref[i * piece : (i + 1) * piece, :] = block
        write_tail(out_ref, wide.size // LANES, norm, base + top_gain, base)


def chain_logs(where, tops, decays, end):
    logs = []
    for k in range(len(where)):
        log = tops[k]
        for o in range(len(where)):
            if o != k:
                between = jnp.logical_and(where[o] > where[k], where[o] < end)
                log = log + jnp.where(between, decays[o], 0.0)
        logs.append(jnp.where(where[k] < end, log, NEG))
    return logs


def chain_sum(where, logs, top, end, refs, at, norms):
    total, norm = 0.0, 0.0
    for k in range(len(where)):
        weight = jnp.where(where[k] < end, jnp.exp(logs[k] - top), 0.0)
        total = total + weight * refs[k][0:at, :].astype(jnp.float32)
        norm = norm + weight * norms[k]
    return total, norm


def group_total_kernel(inner, width_k, *refs):
    ins, out_ref = refs[:-1], refs[-1]
    member = lax.rem(lax.axis_index("ctx"), inner)
    where = [source(member, k, inner) for k in range(inner)]
    at, (norms, tops, decays) = read_tails(ins, width_k)
    logs = chain_logs(where, tops, decays, inner)
    top = functools.reduce(jnp.maximum, logs)
    total, norm = chain_sum(where, logs, top, inner, ins, at, norms)
    out_ref[0:at, :] = total.astype(jnp.bfloat16)
    write_tail(out_ref, at, norm, top, functools.reduce(jnp.add, decays))


def near_kernel(inner, width_k, *refs):
    ins, outs, stats_ref = refs[:inner], refs[inner:-1], refs[-1]
    member = lax.rem(lax.axis_index("ctx"), inner)
    where = [source(member, k, inner) for k in range(inner)]
    at, (norms, tops, decays) = read_tails(ins, width_k)
    for t in range(inner):
        end = target(member, t, inner)
        logs = chain_logs(where, tops, decays, end)
        top = functools.reduce(jnp.maximum, logs)
        total, norm = chain_sum(where, logs, top, end, ins, at, norms)
        outs[t][...] = total
        decay = 0.0
        for k in range(inner):
            decay = decay + jnp.where(where[k] < end, decays[k], 0.0)
        pad = jnp.zeros((8 - norm.shape[0] % 8 - 2, LANES), jnp.float32)
        stats_ref[t, :, :] = jnp.concatenate([top, decay, norm, pad], axis=0)


def far_kernel(inner, outer, width_k, stats_ref, *refs):
    totals, nears = refs[: outer - 1], refs[outer - 1 : outer - 1 + inner]
    outs, state_ref = refs[outer - 1 + inner : -1], refs[-1]
    group = lax.div(lax.axis_index("ctx"), inner)
    where = [source(group, k, outer) for k in far_order(outer)]
    at, (norms, tops, decays) = read_tails(totals, width_k)
    logs = chain_logs(where, tops, decays, group)
    far_top = functools.reduce(jnp.maximum, logs)
    far, far_norm = chain_sum(where, logs, far_top, group, totals, at, norms)
    n = width_k // LANES
    for t in range(inner):
        stats = stats_ref[t, :, :]
        far_log = far_top + stats[1:2]
        top = jnp.maximum(stats[0:1], far_log)
        w_near, w_far = jnp.exp(stats[0:1] - top), jnp.exp(far_log - top)
        outs[t][...] = (w_far * far + w_near * nears[t][...]).astype(jnp.bfloat16)
        if t == 0:
            norm = w_far * far_norm + w_near * stats[2 : 2 + n]
            pad = jnp.zeros((state_ref.shape[0] - 1 - n, LANES), jnp.float32)
            state_ref[...] = jnp.concatenate([top, norm, pad], axis=0)


def inside_kernel(gates_ref, output_ref, queries_ref, keys_ref, values_ref, num_ref, stats_ref):
    rows = queries_ref.shape[0] // LANES
    scale = queries_ref.shape[1] ** (-0.5)
    across = lax.broadcasted_iota(jnp.int32, (LANES, LANES), 1)
    causal = lax.broadcasted_iota(jnp.int32, (LANES, LANES), 0) >= across
    gain = gates_ref[0:rows, :]
    stats_ref[2 * rows : 3 * rows, :] = jax.nn.sigmoid(output_ref[...])
    before = jnp.full((1, 1), NEG, jnp.float32)
    for i in range(rows):
        here = slice(i * LANES, (i + 1) * LANES)
        a_row = gain[i : i + 1]
        peak = jnp.max(jnp.where(causal, a_row, NEG), axis=1, keepdims=True)
        peak = jnp.maximum(peak, before)
        before = jnp.maximum(before, jnp.max(a_row, axis=1, keepdims=True))
        width = (i + 1) * LANES
        scores = lax.dot_general(
            queries_ref[here, :],
            keys_ref[0:width, :],
            (((1,), (1,)), ((), ())),
            preferred_element_type=jnp.float32,
        )
        parts, den = [], 0.0
        for j in range(i + 1):
            diff = gain[j : j + 1] - peak
            if j == i:
                diff = jnp.where(causal, diff, NEG)
            part = jnp.exp(diff) * (scores[:, j * LANES : (j + 1) * LANES] * scale)
            den = den + part
            parts.append(part.astype(jnp.bfloat16))
        weighted = parts[0] if i == 0 else jnp.concatenate(parts, axis=1)
        den = jnp.sum(den, axis=1, keepdims=True)
        num_ref[here, :] = jnp.dot(
            weighted, values_ref[0:width, :], preferred_element_type=jnp.float32
        )
        turned = jnp.where(across == 0, den, peak).T
        stats_ref[i : i + 1, :] = turned[0:1]
        stats_ref[rows + i : rows + i + 1, :] = turned[1:2]


def rescale_kernel(state_ref, gates_ref, stats_ref, queries_ref, num_ref, done_ref, lift_ref):
    rows, width = gates_ref.shape[0] // 2, queries_ref.shape[1]
    n = width // LANES
    scale = width ** (-0.5)
    top_prev = state_ref[0:1, :]
    norm = jnp.concatenate([state_ref[1 + i : 2 + i, :] for i in range(n)], axis=1)
    three = [p.astype(jnp.float32) for p in pieces3(norm)]
    three.append(jnp.zeros((TILE - 3, width), jnp.float32))
    den_out = lax.dot_general(
        jnp.concatenate(three, axis=0).astype(jnp.bfloat16),
        queries_ref[...],
        (((1,), (1,)), ((), ())),
        preferred_element_type=jnp.float32,
    )
    den_out = jnp.concatenate(lane_blocks(den_out[0:1] + den_out[1:2] + den_out[2:3]), axis=0)
    den_in, peak = stats_ref[0:rows, :], stats_ref[rows : 2 * rows, :]
    top = jnp.maximum(peak, top_prev)
    keep, lift = jnp.exp(peak - top), jnp.exp(top_prev - top) * scale
    den = jnp.abs(keep * den_in + lift * den_out)
    floor = jnp.exp(-(gates_ref[rows : 2 * rows, :] + top))
    ratio = stats_ref[2 * rows : 3 * rows, :] / jnp.maximum(den, floor)
    keep, lift = keep * ratio, lift * ratio
    for i in range(rows):
        here = slice(i * LANES, (i + 1) * LANES)
        column = jnp.broadcast_to(keep[i : i + 1], (LANES, LANES)).T
        for j in range(num_ref.shape[1] // LANES):
            there = slice(j * LANES, (j + 1) * LANES)
            done_ref[here, there] = column * num_ref[here, there]
        lift_ref[here, :] = jnp.broadcast_to(lift[i : i + 1], (LANES, LANES)).T


def output_kernel(inner, queries_ref, done_ref, lift_ref, *rest):
    pieces, (out_ref, memory) = rest[:inner], rest[inner:]
    member = lax.rem(lax.axis_index("ctx"), inner)
    piece = memory.shape[0] // inner
    for k in range(inner):
        start = pl.multiple_of(source(member, k, inner) * piece, piece)
        for i in range(memory.shape[1] // LANES):
            memory[pl.ds(start, piece), i * LANES : (i + 1) * LANES] = pieces[k][
                i * piece : (i + 1) * piece, :
            ]
    for i in range(queries_ref.shape[0] // LANES):
        here = slice(i * LANES, (i + 1) * LANES)
        num_out = jnp.dot(queries_ref[here, :], memory[...], preferred_element_type=jnp.float32)
        column = lift_ref[here, :]
        for j, block in enumerate(lane_blocks(num_out)):
            there = slice(j * LANES, (j + 1) * LANES)
            out_ref[here, there] = (done_ref[here, there] + column * block).astype(jnp.bfloat16)


def own_kernel(heads, orders, rows, gated_ref, *refs):
    bufs, (part_ref, other_ref, mine) = refs[:-3], refs[-3:]
    place, head = lax.axis_index("ctx"), lax.axis_index("head")
    width = mine.shape[0]
    each = width // rows
    at = 0
    for buf in bufs:
        for s in range(buf.shape[0] // rows):
            even, odd = (order[at] for order in orders)
            block = place ^ (even if even == odd else jnp.where(head % 2 == 0, even, odd))
            owner, start = lax.div(block, each), pl.multiple_of(lax.rem(block, each) * rows, rows)
            here = buf.at[s * rows : (s + 1) * rows, :]

            @pl.when(owner == head)
            def _():
                mine[pl.ds(start, rows), :] = here[...]

            @pl.when(owner != head)
            def _():
                away = (exchange(head, owner, heads) - 1) * width + start
                other_ref[pl.ds(pl.multiple_of(away, rows), rows), :] = here[...]

            at += 1
    part_ref[...] = jnp.dot(gated_ref[...], mine[...], preferred_element_type=jnp.float32)


def others_kernel(part_ref, other_ref, *refs):
    gated, (out_hbm, held, sems) = refs[:-3], refs[-3:]
    width = gated[0].shape[1]
    steps, rows = held.shape[:2]
    copies = []
    for c in range(steps):
        here = slice(c * rows, (c + 1) * rows)
        total = part_ref[here, :]
        for k, g in enumerate(gated):
            part = other_ref[k * width : (k + 1) * width, :]
            total = total + jnp.dot(g[here, :], part, preferred_element_type=jnp.float32)
        held[c, :, :] = total.astype(jnp.bfloat16)
        copies.append(
            pltpu.make_async_copy(held.at[c], out_hbm.at[pl.ds(c * rows, rows), :], sems.at[c])
        )
        copies[-1].start()
    for copy in copies:
        copy.wait()


def join_kernel(*refs):
    out_ref, at = refs[-1], 0
    for ref in refs[:-1]:
        out_ref[at : at + ref.shape[0], :] = ref[...]
        at += ref.shape[0]


def call(kernel, out_shape, args, scratch=(), micros=1.0, after=(), plain=(), to_hbm=False):
    skip = len(after)
    anywhere, hbm, vmem = (
        pl.BlockSpec(memory_space=m) for m in (pl.ANY, pltpu.HBM, pltpu.VMEM)
    )
    return pl.pallas_call(
        lambda *refs: kernel(*refs[skip:]),
        out_shape=out_shape,
        in_specs=[anywhere] * skip + [hbm if i in plain else vmem for i in range(len(args))],
        out_specs=jax.tree.map(lambda _: hbm if to_hbm else vmem, out_shape),
        scratch_shapes=scratch,
        compiler_params=pltpu.CompilerParams(vmem_limit_bytes=24 * 2**20),
        cost_estimate=pl.CostEstimate(
            flops=int(micros * 1.1e9), bytes_accessed=int(micros * 3.7e6), transcendentals=0
        ),
    )(*after, *args)


def shape(dims, dtype):
    return jax.ShapeDtypeStruct(dims, dtype)


def join(parts, after=(), micros=0.5):
    out = shape((sum(p.shape[0] for p in parts), parts[0].shape[1]), parts[0].dtype)
    return call(join_kernel, out, parts, micros=micros, after=after)


def doubling_steps(n_ctx):
    assert is_pow2(n_ctx) and n_ctx >= 16
    return [1 << b for b in reversed(range(2, n_ctx.bit_length() - 1))]


def local(n_ctx, n_head, queries, keys, values, input_pre, forget_pre, output_pre, w_out):
    tok, width_k = queries.shape
    width_v = values.shape[1]
    inner, outer = split_groups(n_ctx)
    piece = width_k // inner
    bf16, f32 = jnp.bfloat16, jnp.float32
    gate_rows = tok // LANES
    forget, gate_in, gate_out = (
        g.reshape(gate_rows, LANES) for g in (forget_pre, input_pre, output_pre)
    )
    memory_rows = piece * width_v // LANES
    message = shape((memory_rows + rows_for(width_k), LANES), bf16)

    def over_ctx(held, even, odd):
        pairs = [
            (j * n_head + h, (j ^ (odd if h % 2 else even)) * n_head + h)
            for j in range(n_ctx)
            for h in range(n_head)
        ]
        return lax.ppermute(held, ("ctx", "head"), pairs)

    def in_group(sent):
        return sent[:1] + [
            lax.ppermute(sent[k], "ctx", inner_pairs(n_ctx, inner, k)) for k in range(1, inner)
        ]

    *steps, last = doubling_steps(n_ctx)
    order, halves = [0], [w_out]
    for step in steps:
        held = halves[0] if len(halves) == 1 else join(halves)
        halves = [held, over_ctx(held, step, step)]
        order.extend([x ^ step for x in order])

    gates, *sends = call(
        functools.partial(summary_kernel, inner),
        [shape((2 * gate_rows, LANES), f32)] + [message] * inner,
        [
            pltpu.with_memory_space_constraint(x, pltpu.HBM)
            for x in (forget, gate_in, keys, values)
        ],
        [
            pltpu.VMEM((width_k, width_v), bf16),
            *[pltpu.VMEM(x.shape, x.dtype) for x in (forget, gate_in, keys, values)],
            pltpu.SemaphoreType.DMA((4,)),
        ],
        micros=2.0,
        plain=(0, 1, 2, 3),
    )
    blocks = in_group(sends)

    one, other = (1, 2), (2, 1)
    early = join(halves, [gates])
    late = over_ctx(early, last, last)
    first_early = over_ctx(early, *one)
    waited = join([gates], [early], 8.0)
    total = call(
        functools.partial(group_total_kernel, inner, width_k), message, blocks, after=[waited]
    )
    totals = [
        lax.ppermute(total, "ctx", outer_pairs(n_ctx, inner, k)) for k in far_order(outer)
    ]
    late = join([late], [total])
    first_late = over_ctx(late, *one)
    *nears, stats = call(
        functools.partial(near_kernel, inner, width_k),
        [shape((memory_rows, LANES), f32)] * inner + [shape((inner, 8, LANES), f32)],
        blocks,
        micros=8.0,
        after=[late],
    )
    held = join([early, late], [stats])
    second = over_ctx(held, *other)
    third_early = over_ctx(join([first_early], [stats]), *other)
    third_late = over_ctx(first_late, *other)
    orders = []
    for a, b in zip(one, other):
        halves = [order, [x ^ last for x in order]]
        orders.append(
            [x ^ s for s in (0, b) for half in halves for x in half]
            + [x ^ s for half in halves for s in (a, a ^ b) for x in half]
        )

    *prefixes, state = call(
        functools.partial(far_kernel, inner, outer, width_k),
        [shape((memory_rows, LANES), bf16)] * inner + [shape((8, LANES), f32)],
        (stats, *totals, *nears),
        micros=8.0,
        after=[held],
    )
    parts = in_group(prefixes)
    num_in, stats_in = call(
        inside_kernel,
        [shape((tok, width_v), f32), shape((3 * gate_rows, LANES), f32)],
        (gates, gate_out, queries, keys, values),
        micros=8.0,
        after=[state, third_early],
    )
    done, lift = call(
        rescale_kernel,
        [shape((tok, width_v), f32), shape((tok, LANES), f32)],
        (state, gates, stats_in, queries, num_in),
        micros=8.0,
        after=[first_late, third_early],
    )
    gated = call(
        functools.partial(output_kernel, inner),
        shape((tok, width_v), bf16),
        (queries, done, lift, *parts),
        [pltpu.VMEM((width_k, width_v), bf16)],
        micros=0.1,
        after=[second],
    )
    others = [
        lax.ppermute(gated, "head", [(j, target(j, k, n_head)) for j in range(n_head)])
        for k in range(1, n_head)
    ]
    cols_out = w_out.shape[1]
    part, other_rows = call(
        functools.partial(own_kernel, n_head, orders, w_out.shape[0]),
        [shape((tok, cols_out), f32), shape(((n_head - 1) * width_v, cols_out), bf16)],
        (gated, held, second, first_early, third_early, first_late, third_late),
        [pltpu.VMEM((width_v, cols_out), bf16)],
        micros=5.0,
    )
    return call(
        others_kernel,
        shape((tok, cols_out), bf16),
        (part, other_rows, *others),
        [
            pltpu.VMEM((gate_rows, LANES, cols_out), bf16),
            pltpu.SemaphoreType.DMA((gate_rows,)),
        ],
        micros=1.0,
        to_hbm=True,
    )


def solution(mesh):
    spec = P("ctx", "head")
    return jax.shard_map(
        functools.partial(local, mesh.shape["ctx"], mesh.shape["head"]),
        mesh=mesh,
        in_specs=(spec,) * 7,
        out_specs=spec,
        check_vma=False,
    )
```

```python
import functools

import jax
import jax.numpy as jnp
from jax import lax
from jax.experimental import pallas as pl
from jax.experimental.pallas import tpu as pltpu
from jax.sharding import PartitionSpec as P

TILE = 16
LANES = 128
NEG = -1e30


def split_groups(n):
    inner = max(a for a in range(1, n + 1) if n % a == 0 and a * a <= n)
    return inner, n // inner


def is_pow2(n):
    return n & (n - 1) == 0


def source(i, k, n):
    return i ^ (-k % n) if is_pow2(n) else (i + k) % n


def target(i, k, n):
    return i ^ (-k % n) if is_pow2(n) else (i + n - k) % n


def exchange(i, j, n):
    return lax.rem(n - (i ^ j) if is_pow2(n) else j + n - i, n)


def inner_pairs(n, inner, k):
    return [(j, j - j % inner + target(j % inner, k, inner)) for j in range(n)]


def far_order(outer):
    order = list(range(1, outer))
    return order[1::-1] + order[2:]


def outer_pairs(n, inner, k):
    outer = n // inner
    return [(j, target(j // inner, k, outer) * inner + j % inner) for j in range(n)]


def pieces3(x):
    hi = x.astype(jnp.bfloat16)
    rest = x - hi.astype(jnp.float32)
    mid = rest.astype(jnp.bfloat16)
    low = (rest - mid.astype(jnp.float32)).astype(jnp.bfloat16)
    return hi, mid, low


def lane_blocks(x):
    return [x[:, i : i + LANES] for i in range(0, x.shape[1], LANES)]


def rows_for(width_k):
    rows = 3 * (width_k // LANES + 2)
    return rows + -rows % TILE


def write_tail(ref, at, norm, top, decay):
    wide = jnp.concatenate([norm] + [jnp.broadcast_to(x, (1, LANES)) for x in (top, decay)], axis=0)
    rows = [p.astype(jnp.float32) for p in pieces3(wide)]
    count = ref.shape[0] - at - 3 * wide.shape[0]
    if count:
        rows.append(jnp.zeros((count, LANES), jnp.float32))
    ref[at:, :] = jnp.concatenate(rows, axis=0).astype(jnp.bfloat16)


def read_tail(ref, at, width_k):
    tail = ref[at:, :].astype(jnp.float32)
    n = width_k // LANES
    tail = tail[0 : n + 2] + tail[n + 2 : 2 * n + 4] + tail[2 * n + 4 : 3 * n + 6]
    return tail[0:n], tail[n : n + 1], tail[n + 1 : n + 2]


def read_tails(refs, width_k):
    at = refs[0].shape[0] - rows_for(width_k)
    return at, zip(*[read_tail(r, at, width_k) for r in refs])


def summary_kernel(inner, *refs):
    given, gates_ref, outs = refs[:4], refs[4], refs[5 : 5 + inner]
    memory, sems = refs[5 + inner], refs[-1]
    held = forget_ref, input_ref, keys_ref, values_ref = refs[6 + inner : -1]
    copies = [
        pltpu.make_async_copy(src, dst, sems.at[i]) for i, (src, dst) in enumerate(zip(given, held))
    ]
    for copy in copies:
        copy.start()
    copies[0].wait()
    copies[1].wait()
    member = lax.rem(lax.axis_index("ctx"), inner)
    rows = forget_ref.shape[0]
    forget = forget_ref[...]
    log_keep = jnp.minimum(forget, 0.0) - jnp.log1p(jnp.exp(-jnp.abs(forget)))
    tri = lax.broadcasted_iota(jnp.int32, (LANES, LANES), 0) <= lax.broadcasted_iota(
        jnp.int32, (LANES, LANES), 1
    )
    parts = jnp.concatenate([p.astype(jnp.float32) for p in pieces3(log_keep)], axis=0)
    sums = jnp.dot(
        parts.astype(jnp.bfloat16),
        tri.astype(jnp.bfloat16),
        preferred_element_type=jnp.float32,
    )
    inside = sums[:rows] + sums[rows : 2 * rows] + sums[2 * rows : 3 * rows]
    base = jnp.zeros((1, 1), jnp.float32)
    cum = []
    for r in range(rows):
        row = inside[r : r + 1]
        cum.append(row + base)
        base = base + row[:, LANES - 1 :]
    cum_decay = jnp.concatenate(cum, axis=0)
    gain = input_ref[...] - cum_decay
    top_gain = jnp.max(jnp.max(gain, axis=1, keepdims=True), axis=0, keepdims=True)
    weight = jnp.exp(gain - top_gain)
    gates_ref[0:rows, :] = gain
    gates_ref[rows : 2 * rows, :] = cum_decay
    along = jnp.concatenate([weight[r : r + 1] for r in range(rows)], axis=1)
    three = [p.astype(jnp.float32) for p in pieces3(along)]
    three.append(jnp.zeros((TILE - 3, along.shape[1]), jnp.float32))
    three = jnp.concatenate(three, axis=0).astype(jnp.bfloat16)
    copies[2].wait()
    keys = keys_ref[...]
    scaled = (keys.astype(jnp.float32).T * along).astype(jnp.bfloat16)
    norms = jnp.dot(three, keys, preferred_element_type=jnp.float32)
    norm = jnp.concatenate(lane_blocks(norms[0:1] + norms[1:2] + norms[2:3]), axis=0)
    copies[3].wait()
    whole = jnp.dot(scaled, values_ref[...], preferred_element_type=jnp.float32)
    memory[...] = whole.astype(jnp.bfloat16)
    piece = memory.shape[0] // inner
    for k, out_ref in enumerate(outs):
        start = pl.multiple_of(target(member, k, inner) * piece, piece)
        wide = memory[pl.ds(start, piece), :]
        for i, block in enumerate(lane_blocks(wide)):
            out_ref[i * piece : (i + 1) * piece, :] = block
        at = wide.size // LANES
        if k == 0:
            write_tail(out_ref, at, norm, base + top_gain, base)
            tail = out_ref[at:, :]
        else:
            out_ref[at:, :] = tail


def chain_logs(where, tops, decays, end):
    logs = []
    for k in range(len(where)):
        log = tops[k]
        for o in range(len(where)):
            if o != k:
                between = jnp.logical_and(where[o] > where[k], where[o] < end)
                log = log + jnp.where(between, decays[o], 0.0)
        logs.append(jnp.where(where[k] < end, log, NEG))
    return logs


def chain_sum(where, logs, top, end, refs, at, norms):
    total, norm = 0.0, 0.0
    for k in range(len(where)):
        weight = jnp.where(where[k] < end, jnp.exp(logs[k] - top), 0.0)
        total = total + weight * refs[k][0:at, :].astype(jnp.float32)
        norm = norm + weight * norms[k]
    return total, norm


def group_total_kernel(inner, width_k, *refs):
    ins, out_ref = refs[:-1], refs[-1]
    member = lax.rem(lax.axis_index("ctx"), inner)
    where = [source(member, k, inner) for k in range(inner)]
    at, (norms, tops, decays) = read_tails(ins, width_k)
    logs = chain_logs(where, tops, decays, inner)
    top = functools.reduce(jnp.maximum, logs)
    total, norm = chain_sum(where, logs, top, inner, ins, at, norms)
    out_ref[0:at, :] = total.astype(jnp.bfloat16)
    write_tail(out_ref, at, norm, top, functools.reduce(jnp.add, decays))


def near_kernel(inner, width_k, *refs):
    ins, outs, stats_ref = refs[:inner], refs[inner:-1], refs[-1]
    member = lax.rem(lax.axis_index("ctx"), inner)
    where = [source(member, k, inner) for k in range(inner)]
    at, (norms, tops, decays) = read_tails(ins, width_k)
    for t in range(inner):
        end = target(member, t, inner)
        logs = chain_logs(where, tops, decays, end)
        top = functools.reduce(jnp.maximum, logs)
        total, norm = chain_sum(where, logs, top, end, ins, at, norms)
        outs[t][...] = total
        decay = 0.0
        for k in range(inner):
            decay = decay + jnp.where(where[k] < end, decays[k], 0.0)
        pad = jnp.zeros((8 - norm.shape[0] % 8 - 2, LANES), jnp.float32)
        stats_ref[t, :, :] = jnp.concatenate([top, decay, norm, pad], axis=0)


def far_kernel(inner, outer, width_k, stats_ref, *refs):
    totals, nears = refs[: outer - 1], refs[outer - 1 : outer - 1 + inner]
    outs, state_ref = refs[outer - 1 + inner : -1], refs[-1]
    group = lax.div(lax.axis_index("ctx"), inner)
    where = [source(group, k, outer) for k in far_order(outer)]
    at, (norms, tops, decays) = read_tails(totals, width_k)
    logs = chain_logs(where, tops, decays, group)
    far_top = functools.reduce(jnp.maximum, logs)
    far, far_norm = chain_sum(where, logs, far_top, group, totals, at, norms)
    n = width_k // LANES
    for t in range(inner):
        stats = stats_ref[t, :, :]
        far_log = far_top + stats[1:2]
        top = jnp.maximum(stats[0:1], far_log)
        w_near, w_far = jnp.exp(stats[0:1] - top), jnp.exp(far_log - top)
        outs[t][...] = (w_far * far + w_near * nears[t][...]).astype(jnp.bfloat16)
        if t == 0:
            norm = w_far * far_norm + w_near * stats[2 : 2 + n]
            pad = jnp.zeros((state_ref.shape[0] - 1 - n, LANES), jnp.float32)
            state_ref[...] = jnp.concatenate([top, norm, pad], axis=0)


def inside_kernel(gates_ref, output_ref, queries_ref, keys_ref, values_ref, num_ref, stats_ref):
    rows = queries_ref.shape[0] // LANES
    scale = queries_ref.shape[1] ** (-0.5)
    across = lax.broadcasted_iota(jnp.int32, (LANES, LANES), 1)
    causal = lax.broadcasted_iota(jnp.int32, (LANES, LANES), 0) >= across
    gain = gates_ref[0:rows, :]
    stats_ref[2 * rows : 3 * rows, :] = jax.nn.sigmoid(output_ref[...])
    before = jnp.full((1, 1), NEG, jnp.float32)
    for i in range(rows):
        here = slice(i * LANES, (i + 1) * LANES)
        a_row = gain[i : i + 1]
        peak = jnp.max(jnp.where(causal, a_row, NEG), axis=1, keepdims=True)
        peak = jnp.maximum(peak, before)
        before = jnp.maximum(before, jnp.max(a_row, axis=1, keepdims=True))
        width = (i + 1) * LANES
        scores = lax.dot_general(
            queries_ref[here, :],
            keys_ref[0:width, :],
            (((1,), (1,)), ((), ())),
            preferred_element_type=jnp.float32,
        )
        parts, den = [], 0.0
        for j in range(i + 1):
            diff = gain[j : j + 1] - peak
            if j == i:
                diff = jnp.where(causal, diff, NEG)
            part = jnp.exp(diff) * (scores[:, j * LANES : (j + 1) * LANES] * scale)
            den = den + part
            parts.append(part.astype(jnp.bfloat16))
        weighted = parts[0] if i == 0 else jnp.concatenate(parts, axis=1)
        den = jnp.sum(den, axis=1, keepdims=True)
        num_ref[here, :] = jnp.dot(
            weighted, values_ref[0:width, :], preferred_element_type=jnp.float32
        )
        turned = jnp.where(across == 0, den, peak).T
        stats_ref[i : i + 1, :] = turned[0:1]
        stats_ref[rows + i : rows + i + 1, :] = turned[1:2]


def rescale_kernel(state_ref, gates_ref, stats_ref, queries_ref, num_ref, done_ref, lift_ref):
    rows, width = gates_ref.shape[0] // 2, queries_ref.shape[1]
    n = width // LANES
    scale = width ** (-0.5)
    top_prev = state_ref[0:1, :]
    norm = jnp.concatenate([state_ref[1 + i : 2 + i, :] for i in range(n)], axis=1)
    three = [p.astype(jnp.float32) for p in pieces3(norm)]
    three.append(jnp.zeros((TILE - 3, width), jnp.float32))
    den_out = lax.dot_general(
        jnp.concatenate(three, axis=0).astype(jnp.bfloat16),
        queries_ref[...],
        (((1,), (1,)), ((), ())),
        preferred_element_type=jnp.float32,
    )
    den_out = jnp.concatenate(lane_blocks(den_out[0:1] + den_out[1:2] + den_out[2:3]), axis=0)
    den_in, peak = stats_ref[0:rows, :], stats_ref[rows : 2 * rows, :]
    top = jnp.maximum(peak, top_prev)
    keep, lift = jnp.exp(peak - top), jnp.exp(top_prev - top) * scale
    den = jnp.abs(keep * den_in + lift * den_out)
    floor = jnp.exp(-(gates_ref[rows : 2 * rows, :] + top))
    ratio = stats_ref[2 * rows : 3 * rows, :] / jnp.maximum(den, floor)
    keep, lift = keep * ratio, lift * ratio
    for i in range(rows):
        here = slice(i * LANES, (i + 1) * LANES)
        column = jnp.broadcast_to(keep[i : i + 1], (LANES, LANES)).T
        for j in range(num_ref.shape[1] // LANES):
            there = slice(j * LANES, (j + 1) * LANES)
            done_ref[here, there] = column * num_ref[here, there]
        lift_ref[here, :] = jnp.broadcast_to(lift[i : i + 1], (LANES, LANES)).T


def output_kernel(inner, queries_ref, done_ref, lift_ref, *rest):
    pieces, (out_ref, memory) = rest[:inner], rest[inner:]
    member = lax.rem(lax.axis_index("ctx"), inner)
    piece = memory.shape[0] // inner
    for k in range(inner):
        start = pl.multiple_of(source(member, k, inner) * piece, piece)
        for i in range(memory.shape[1] // LANES):
            memory[pl.ds(start, piece), i * LANES : (i + 1) * LANES] = pieces[k][
                i * piece : (i + 1) * piece, :
            ]
    for i in range(queries_ref.shape[0] // LANES):
        here = slice(i * LANES, (i + 1) * LANES)
        num_out = jnp.dot(queries_ref[here, :], memory[...], preferred_element_type=jnp.float32)
        column = lift_ref[here, :]
        for j, block in enumerate(lane_blocks(num_out)):
            there = slice(j * LANES, (j + 1) * LANES)
            out_ref[here, there] = (done_ref[here, there] + column * block).astype(jnp.bfloat16)


def own_kernel(heads, orders, rows, gated_ref, *refs):
    bufs, (part_ref, other_ref, mine) = refs[:-3], refs[-3:]
    place, head = lax.axis_index("ctx"), lax.axis_index("head")
    width = mine.shape[0]
    each = width // rows
    at = 0
    for buf in bufs:
        for s in range(buf.shape[0] // rows):
            even, odd = (order[at] for order in orders)
            block = place ^ (even if even == odd else jnp.where(head % 2 == 0, even, odd))
            owner, start = lax.div(block, each), pl.multiple_of(lax.rem(block, each) * rows, rows)
            here = buf.at[s * rows : (s + 1) * rows, :]

            @pl.when(owner == head)
            def _():
                mine[pl.ds(start, rows), :] = here[...]

            @pl.when(owner != head)
            def _():
                away = (exchange(head, owner, heads) - 1) * width + start
                other_ref[pl.ds(pl.multiple_of(away, rows), rows), :] = here[...]

            at += 1
    part_ref[...] = jnp.dot(gated_ref[...], mine[...], preferred_element_type=jnp.float32)


def others_kernel(part_ref, other_ref, *refs):
    gated, (out_hbm, held, sems) = refs[:-3], refs[-3:]
    width = gated[0].shape[1]
    steps, rows = held.shape[:2]
    copies = []
    for c in range(steps):
        here = slice(c * rows, (c + 1) * rows)
        total = part_ref[here, :]
        for k, g in enumerate(gated):
            part = other_ref[k * width : (k + 1) * width, :]
            total = total + jnp.dot(g[here, :], part, preferred_element_type=jnp.float32)
        held[c, :, :] = total.astype(jnp.bfloat16)
        copies.append(
            pltpu.make_async_copy(held.at[c], out_hbm.at[pl.ds(c * rows, rows), :], sems.at[c])
        )
        copies[-1].start()
    for copy in copies:
        copy.wait()


def join_kernel(*refs):
    out_ref, at = refs[-1], 0
    for ref in refs[:-1]:
        out_ref[at : at + ref.shape[0], :] = ref[...]
        at += ref.shape[0]


def call(kernel, out_shape, args, scratch=(), micros=1.0, after=(), plain=(), to_hbm=False):
    skip = len(after)
    anywhere, hbm, vmem = (
        pl.BlockSpec(memory_space=m) for m in (pl.ANY, pltpu.HBM, pltpu.VMEM)
    )
    return pl.pallas_call(
        lambda *refs: kernel(*refs[skip:]),
        out_shape=out_shape,
        in_specs=[anywhere] * skip + [hbm if i in plain else vmem for i in range(len(args))],
        out_specs=jax.tree.map(lambda _: hbm if to_hbm else vmem, out_shape),
        scratch_shapes=scratch,
        compiler_params=pltpu.CompilerParams(vmem_limit_bytes=24 * 2**20),
        cost_estimate=pl.CostEstimate(
            flops=int(micros * 1.1e9), bytes_accessed=int(micros * 3.7e6), transcendentals=0
        ),
    )(*after, *args)


def shape(dims, dtype):
    return jax.ShapeDtypeStruct(dims, dtype)


def join(parts, after=(), micros=0.5):
    out = shape((sum(p.shape[0] for p in parts), parts[0].shape[1]), parts[0].dtype)
    return call(join_kernel, out, parts, micros=micros, after=after)


def doubling_steps(n_ctx):
    assert is_pow2(n_ctx) and n_ctx >= 16
    return [1 << b for b in reversed(range(2, n_ctx.bit_length() - 1))]


def local(n_ctx, n_head, queries, keys, values, input_pre, forget_pre, output_pre, w_out):
    tok, width_k = queries.shape
    width_v = values.shape[1]
    inner, outer = split_groups(n_ctx)
    piece = width_k // inner
    bf16, f32 = jnp.bfloat16, jnp.float32
    gate_rows = tok // LANES
    forget, gate_in, gate_out = (
        g.reshape(gate_rows, LANES) for g in (forget_pre, input_pre, output_pre)
    )
    memory_rows = piece * width_v // LANES
    message = shape((memory_rows + rows_for(width_k), LANES), bf16)

    def over_ctx(held, even, odd):
        pairs = [
            (j * n_head + h, (j ^ (odd if h % 2 else even)) * n_head + h)
            for j in range(n_ctx)
            for h in range(n_head)
        ]
        return lax.ppermute(held, ("ctx", "head"), pairs)

    def in_group(sent):
        return sent[:1] + [
            lax.ppermute(sent[k], "ctx", inner_pairs(n_ctx, inner, k)) for k in range(1, inner)
        ]

    *steps, last = doubling_steps(n_ctx)
    order, halves = [0], [w_out]
    for step in steps:
        held = halves[0] if len(halves) == 1 else join(halves)
        halves = [held, over_ctx(held, step, step)]
        order.extend([x ^ step for x in order])

    gates, *sends = call(
        functools.partial(summary_kernel, inner),
        [shape((2 * gate_rows, LANES), f32)] + [message] * inner,
        [
            pltpu.with_memory_space_constraint(x, pltpu.HBM)
            for x in (forget, gate_in, keys, values)
        ],
        [
            pltpu.VMEM((width_k, width_v), bf16),
            *[pltpu.VMEM(x.shape, x.dtype) for x in (forget, gate_in, keys, values)],
            pltpu.SemaphoreType.DMA((4,)),
        ],
        micros=2.0,
        plain=(0, 1, 2, 3),
    )
    blocks = in_group(sends)

    one, other = (1, 2), (2, 1)
    early = join(halves, [gates])
    late = over_ctx(early, last, last)
    first_early = over_ctx(early, *one)
    waited = join([gates], [early], 8.0)
    total = call(
        functools.partial(group_total_kernel, inner, width_k), message, blocks, after=[waited]
    )
    totals = [
        lax.ppermute(total, "ctx", outer_pairs(n_ctx, inner, k)) for k in far_order(outer)
    ]
    late = join([late], [total])
    first_late = over_ctx(late, *one)
    *nears, stats = call(
        functools.partial(near_kernel, inner, width_k),
        [shape((memory_rows, LANES), f32)] * inner + [shape((inner, 8, LANES), f32)],
        blocks,
        micros=8.0,
        after=[late],
    )
    held = join([early, late], [stats])
    second = over_ctx(held, *other)
    third_early = over_ctx(join([first_early], [stats]), *other)
    third_late = over_ctx(first_late, *other)
    orders = []
    for a, b in zip(one, other):
        halves = [order, [x ^ last for x in order]]
        orders.append(
            [x ^ s for s in (0, b) for half in halves for x in half]
            + [x ^ s for half in halves for s in (a, a ^ b) for x in half]
        )

    *prefixes, state = call(
        functools.partial(far_kernel, inner, outer, width_k),
        [shape((memory_rows, LANES), bf16)] * inner + [shape((8, LANES), f32)],
        (stats, *totals, *nears),
        micros=8.0,
        after=[held],
    )
    parts = in_group(prefixes)
    num_in, stats_in = call(
        inside_kernel,
        [shape((tok, width_v), f32), shape((3 * gate_rows, LANES), f32)],
        (gates, gate_out, queries, keys, values),
        micros=8.0,
        after=[state, third_early],
    )
    done, lift = call(
        rescale_kernel,
        [shape((tok, width_v), f32), shape((tok, LANES), f32)],
        (state, gates, stats_in, queries, num_in),
        micros=8.0,
        after=[first_late, third_early],
    )
    gated = call(
        functools.partial(output_kernel, inner),
        shape((tok, width_v), bf16),
        (queries, done, lift, *parts),
        [pltpu.VMEM((width_k, width_v), bf16)],
        micros=0.1,
        after=[second],
    )
    others = [
        lax.ppermute(gated, "head", [(j, target(j, k, n_head)) for j in range(n_head)])
        for k in range(1, n_head)
    ]
    cols_out = w_out.shape[1]
    part, other_rows = call(
        functools.partial(own_kernel, n_head, orders, w_out.shape[0]),
        [shape((tok, cols_out), f32), shape(((n_head - 1) * width_v, cols_out), bf16)],
        (gated, held, second, first_early, third_early, first_late, third_late),
        [pltpu.VMEM((width_v, cols_out), bf16)],
        micros=5.0,
    )
    return call(
        others_kernel,
        shape((tok, cols_out), bf16),
        (part, other_rows, *others),
        [
            pltpu.VMEM((gate_rows, LANES, cols_out), bf16),
            pltpu.SemaphoreType.DMA((gate_rows,)),
        ],
        micros=1.0,
        to_hbm=True,
    )


def solution(mesh):
    spec = P("ctx", "head")
    return jax.shard_map(
        functools.partial(local, mesh.shape["ctx"], mesh.shape["head"]),
        mesh=mesh,
        in_specs=(spec,) * 7,
        out_specs=spec,
        check_vma=False,
    )
```
